128 devices in a mesh: item: 16 (over z, y), code: 8 (over x, core).
Axes of the slice: x: 4, y: 4, z: 4, core: 2. Of those that a mesh axis runs over, the one named last changes fastest.
Arguments:
- residuals: float32 [256, 65536], P('code', 'item'), may hold values from -6 to 6
- codebook: float32 [256, 65536], P('item', 'code'), may hold values from -6 to 6
- item_weight: float32 [65536], P('item'), may hold values from 1 to 100
- code_capacity: float32 [65536], P('code'), may hold values from 0.25 to 4
- pairs: int32 [1024, 128], P('item', 'code'), may hold values from -1 to 127, as said below
Outputs:
- item_potential: float32 [65536], P('item')
- code_potential: float32 [65536], P('code')
The draws below stay inside these ranges and needn't reach their ends.
Inputs may be any that keep to these rules, and one draw needn't show every extreme that they name: `pairs`: each entry is -1 (no candidate) or a code block's number within the code shard of its slot column. Within one item block and one code shard the live entries are distinct, the first slot is always live, and between 1 and 8 are live; some device holds exactly 8 live slots in every item block. Every code block is named by some item block.
All inputs are finite; a program needn't handle non-finite values.
Results may differ from the reference program's by a relative error of at most 0.0003.
Values sent between devices are 32-bit elements; how exact they have to be, the bound alone decides.
A program may use at most 128 MiB of HBM per device.

```python
import math
import jax
import jax.numpy as jnp
from jax import lax

RESIDUAL_WIDTH = 256
BLOCK = 64
ITEM_DEV = 4096
CODE_DEV = 8192
SLOTS_DEV = 16
ITERS = 3
ITEMS = 65536
CODES = 65536
N_CODE = 8


def draw_pairs(key, part):
    item_blocks = ITEMS // BLOCK
    code_shards = CODES // CODE_DEV
    local_blocks = CODE_DEV // BLOCK
    half_slots = SLOTS_DEV // 2
    key_shift = jax.random.fold_in(key, 11)
    key_offset = jax.random.fold_in(key, 12)
    key_count = jax.random.fold_in(key, 13)
    key_heavy = jax.random.fold_in(key, 14)
    key_rank = jax.random.fold_in(key, 15)
    shift = jax.random.randint(key_shift, (1, code_shards), 0, local_blocks)
    base_ids = (jnp.arange(item_blocks, dtype=jnp.int32)[:, None] + shift) % local_blocks
    offset_keys = jax.random.split(key_offset, item_blocks * code_shards)
    offsets = jax.vmap(lambda one_key: jax.random.permutation(one_key, local_blocks - 1)[:SLOTS_DEV - 1])(offset_keys) + 1
    offsets = offsets.reshape(item_blocks, code_shards, SLOTS_DEV - 1).astype(jnp.int32)
    step_ids = jnp.concatenate([jnp.zeros((item_blocks, code_shards, 1), jnp.int32), offsets], axis=-1)
    block_ids = (base_ids[..., None] + step_ids) % local_blocks
    counts = jax.random.randint(key_count, (item_blocks, code_shards), 1, half_slots + 1)
    heavy_keys = jax.random.split(key_heavy, 2)
    heavy_item = jax.random.randint(heavy_keys[0], (), 0, ITEMS // ITEM_DEV)
    heavy_code = jax.random.randint(heavy_keys[1], (), 0, code_shards)
    block_shard = jnp.arange(item_blocks, dtype=jnp.int32) // (ITEM_DEV // BLOCK)
    heavy = (block_shard[:, None] == heavy_item) & (jnp.arange(code_shards, dtype=jnp.int32)[None, :] == heavy_code)
    counts = jnp.where(heavy, half_slots, counts)
    rank_keys = jax.random.split(key_rank, item_blocks * code_shards)
    ranks = jax.vmap(lambda one_key: jax.random.permutation(one_key, SLOTS_DEV - 1))(rank_keys)
    ranks = ranks.reshape(item_blocks, code_shards, SLOTS_DEV - 1)
    is_live = jnp.concatenate([jnp.ones((item_blocks, code_shards, 1), bool), ranks < (counts - 1)[..., None]], axis=-1)
    chosen = jnp.where(is_live, block_ids, -1)
    return chosen.reshape(item_blocks, code_shards * SLOTS_DEV).astype(jnp.int32)


def levels(rng, dims, shards, least, top_value):
    level, own = 1.0, jax.random.fold_in(rng, 6)
    for position, shards_of in shards:
        steps = jnp.exp(jax.random.uniform(jax.random.fold_in(own, position), (shards_of,), jnp.float32, least / len(shards), top_value / len(shards)))
        level = level * jnp.repeat(steps, dims[position] // shards_of).reshape([-1 if axis == position else 1 for axis in range(len(dims))])
    return level


def noise(own_key, shape, width, most, shards=(), kind=jnp.bfloat16):
    drawn = width * jax.random.normal(own_key, shape, jnp.float32)
    if shards:
        drawn = drawn * levels(own_key, shape, shards, -0.22, 0.18)
    return jnp.clip(drawn, -most, most).astype(kind)


def setup_inputs(seed: int = 0) -> dict:
    streams_of = jax.random.split(jax.random.key(seed), 6)
    residuals = noise(streams_of[0], (RESIDUAL_WIDTH, ITEMS), 1.0, 6.0, ((0, 8), (1, 16)), jnp.float32)
    codebook = noise(streams_of[1], (RESIDUAL_WIDTH, CODES), 1.0, 6.0, ((0, 16), (1, 8)), jnp.float32)
    item_weight = jnp.clip(jnp.exp(math.log(100.0) - 4.6051702 * jax.random.uniform(streams_of[2], (ITEMS,), jnp.float32) ** levels(streams_of[2], (ITEMS,), ((0, 16),), -0.2, 0.2)), 1.0, 100.0)
    code_capacity = jnp.clip(jnp.exp(math.log(4.0) - 2.7725887 * jax.random.uniform(streams_of[3], (CODES,), jnp.float32) ** levels(streams_of[3], (CODES,), ((0, 8),), -0.2, 0.2)), 0.25, 4.0)
    pairs = draw_pairs(jax.random.fold_in(streams_of[5], 71), 0)
    return {"residuals": residuals, "codebook": codebook, "item_weight": item_weight, "code_capacity": code_capacity, "pairs": pairs}


masked_score = -1e+30
softness_factor = 0.1

def reference(residuals, codebook, item_weight, code_capacity, pairs):
    item_blocks = ITEMS // BLOCK
    code_blocks = CODES // BLOCK
    local_blocks = CODE_DEV // BLOCK
    half_slots = SLOTS_DEV // 2
    logit_scale = 1.0 / (softness_factor * math.sqrt(RESIDUAL_WIDTH))
    item_logmass = jnp.log(item_weight) - jnp.log(jnp.sum(item_weight))
    code_logmass = jnp.log(code_capacity) - jnp.log(jnp.sum(code_capacity))
    logmass_blocks = item_logmass.reshape(item_blocks, BLOCK)
    grouped = pairs.reshape(item_blocks, N_CODE, SLOTS_DEV)
    order = jnp.argsort((grouped < 0).astype(jnp.int32), axis=2, stable=True)[:, :, :half_slots]
    packed = jnp.take_along_axis(grouped, order.astype(jnp.int32), axis=2)
    live_grouped = packed >= 0
    shard_base = (jnp.arange(N_CODE, dtype=jnp.int32) * local_blocks)[None, :, None]
    global_ids = jnp.where(live_grouped, packed + shard_base, 0).reshape(item_blocks, N_CODE * half_slots).astype(jnp.int32)
    is_live = live_grouped.reshape(item_blocks, N_CODE * half_slots)
    target = jnp.where(is_live, global_ids, code_blocks).astype(jnp.int32)
    catalogue_rows = residuals.T.reshape(item_blocks, BLOCK, RESIDUAL_WIDTH)
    code_rows = codebook.T.reshape(code_blocks, BLOCK, RESIDUAL_WIDTH)

    def tile_scores(block_index):
        picked = code_rows[global_ids[block_index]]
        scores = jnp.einsum('ir,sjr->sij', catalogue_rows[block_index], picked, precision=lax.Precision.HIGHEST) * logit_scale
        return jnp.where(is_live[block_index][:, None, None], scores, masked_score)
    block_range = jnp.arange(item_blocks, dtype=jnp.int32)
    code_potential = jnp.zeros((CODES,), jnp.float32)
    item_potential = jnp.zeros((ITEMS,), jnp.float32)
    for sweep in range(ITERS):
        code_split = code_potential.reshape(code_blocks, BLOCK)

        def block_pass(block_index):
            tiles = tile_scores(block_index)
            logits = tiles + code_split[global_ids[block_index]][:, None, :]
            row_peak = lax.optimization_barrier(jnp.max(logits, axis=(0, 2)))
            row_total = lax.optimization_barrier(jnp.sum(jnp.exp(logits - row_peak[None, :, None]), axis=(0, 2)))
            block_potential = logmass_blocks[block_index] - (row_peak + jnp.log(row_total))
            col_logits = tiles + block_potential[None, :, None]
            block_peak = lax.optimization_barrier(jnp.max(col_logits, axis=1))
            block_total = lax.optimization_barrier(jnp.sum(jnp.exp(col_logits - block_peak[:, None, :]), axis=1))
            live_row = is_live[block_index][:, None]
            return (block_potential, jnp.where(live_row, block_peak, masked_score), jnp.where(live_row, block_total, 0.0))
        potential_blocks, tile_peak, tile_total = lax.map(block_pass, block_range)
        item_potential = potential_blocks.reshape(ITEMS)
        flat_target = target.reshape(-1)
        peak_flat = tile_peak.reshape(-1, BLOCK)
        total_flat = tile_total.reshape(-1, BLOCK)
        col_peak = jnp.full((code_blocks + 1, BLOCK), masked_score, dtype=jnp.float32).at[flat_target].max(peak_flat)
        spread = total_flat * jnp.exp(peak_flat - col_peak[flat_target])
        col_total = jnp.zeros((code_blocks + 1, BLOCK), jnp.float32).at[flat_target].add(spread)
        col_lse = (col_peak[:code_blocks] + jnp.log(col_total[:code_blocks])).reshape(CODES)
        code_potential = code_logmass - col_lse
    return (item_potential, code_potential)
```

```python
import functools
import math

import jax
import jax.numpy as jnp
from jax import lax
from jax.experimental import pallas as pl
from jax.experimental.pallas import tpu as pltpu
from jax.sharding import PartitionSpec as P

BLOCK = 64
SLOTS = 8
KP = SLOTS // 2
NEG = -1e30
SOFTNESS = 0.1
MESH = pl.DeviceIdType.MESH
HIGHEST = lax.Precision.HIGHEST


def kernel(
    cb_ref,
    res_ref,
    wt_ref,
    cap_ref,
    tgt_ref,
    tgtt_ref,
    ids_ref,
    fout_ref,
    gout_ref,
    cg,
    rg,
    vh,
    vl,
    rt,
    s_ref,
    tm_ref,
    ts_ref,
    xrow,
    xy,
    xz,
    csend,
    crecv,
    rsend,
    rrecv,
    lsem,
    rowsend,
    rowrecv,
    ysend,
    yrecv,
    zsend,
    zrecv,
):
    item = lax.axis_index("item")
    code = lax.axis_index("code")
    z, y = item // 4, item % 4
    x, core = code // 2, code % 2
    cd = cg.shape[3]
    idv = rg.shape[2]
    width = 256
    scale = 1.0 / (SOFTNESS * math.sqrt(width))

    def at(zz, yy):
        return {"item": (zz % 4) * 4 + yy % 4, "code": code}

    def ac(cc):
        return {"item": item, "code": cc}

    bar = pltpu.get_barrier_semaphore()
    for d in range(1, 4):
        pl.semaphore_signal(bar, inc=1, device_id=at(z, y + d), device_id_type=MESH)
        pl.semaphore_signal(bar, inc=1, device_id=at(z + d, y), device_id_type=MESH)
    for d in range(1, 8):
        pl.semaphore_signal(bar, inc=1, device_id=ac((code + d) % 8), device_id_type=MESH)
    pl.semaphore_wait(bar, 13)

    half = cd // 2
    LO, HI = slice(0, half), slice(half, cd)
    sends = []

    def put(src, dst, ss, rs, dev):
        c = pltpu.make_async_remote_copy(
            src_ref=src, dst_ref=dst, send_sem=ss, recv_sem=rs, device_id=dev, device_id_type=MESH
        )
        c.start()
        sends.append(c)
        return c

    def place(h, p, s):
        zz, yy = (s, p) if h == 0 else (p, s)
        return (zz % 4) * 4 + yy % 4

    def where_to(h, p, s):
        zz, yy = (s, p) if h == 0 else (p, s)
        return at(zz, yy)

    pos = [(y, z), (z, y)]
    cnt = [0]

    def piece(h, p, s, cols=None, own=False):
        if own:
            return cb_ref.at[h]
        d = place(h, p, s)
        if cols is None:
            return cg.at[d, h]
        return cg.at[d, h, :, pl.ds(cols.start, cols.stop - cols.start)]

    def cput(h, src_ps, cols, to, own=False):
        i = cnt[0]
        cnt[0] += 1
        src = piece(h, *src_ps, cols, own)
        dst = piece(h, *src_ps, cols)
        return put(src, dst, csend.at[i], crecv.at[i], where_to(h, *to))

    prim, sec = {}, {}
    locals_ = []
    for h in range(2):
        p, s = pos[h]
        prim[h, 1] = cput(h, (p, s), None, (p + 1, s), True)
        prim[h, -1] = cput(h, (p, s), None, (p - 1, s), True)
        sec[h, 0, 1] = cput(h, (p, s), None, (p, s + 1), True)
        sec[h, 0, -1] = cput(h, (p, s), None, (p, s - 1), True)
        lc = pltpu.make_async_copy(cb_ref.at[h], cg.at[item, h], lsem.at[h])
        lc.start()
        locals_.append(lc)

    rhalf = idv // 2
    rcnt = [0]

    def rdev(xx):
        return (xx % 4) * 2 + core

    def rput(xx, cols, to, own=False):
        i = rcnt[0]
        rcnt[0] += 1
        d = rdev(xx)
        if cols is None:
            dst = rg.at[d]
        else:
            dst = rg.at[d, :, pl.ds(cols * rhalf, rhalf)]
        return put(res_ref if own else dst, dst, rsend.at[i], rrecv.at[i], ac(to))

    other = x * 2 + (1 - core)
    rp = {}
    rp[1] = rput(x, None, rdev(x + 1), True)
    rp[-1] = rput(x, None, rdev(x - 1), True)
    rc = [rput(x, None, other, True)]
    lc = pltpu.make_async_copy(res_ref, rg.at[code], lsem.at[2])
    lc.start()
    locals_.append(lc)

    ph, sh = {}, {}
    for d in (1, -1):
        for h in range(2):
            p, s = pos[h]
            prim[h, d].wait_recv()
            ph[h, d] = cput(h, (p - d, s), LO if d > 0 else HI, (p + d, s))
            sec[h, d, 1] = cput(h, (p - d, s), None, (p, s + 1))
            sec[h, d, -1] = cput(h, (p - d, s), None, (p, s - 1))
        rp[d].wait_recv()
        rp[2 * d] = rput(x - d, 0 if d > 0 else 1, rdev(x + d))
        rc.append(rput(x - d, None, other))
        for h in range(2):
            p, s = pos[h]
            sec[h, 0, d].wait_recv()
            sh[h, 0, d] = cput(h, (p, s - d), LO if d > 0 else HI, (p, s + d))
    for h in range(2):
        p, s = pos[h]
        ph[h, 1].wait_recv()
        ph[h, -1].wait_recv()
        sec[h, 2, 1] = cput(h, (p + 2, s), None, (p, s + 1))
        sec[h, 2, -1] = cput(h, (p + 2, s), None, (p, s - 1))
    rp[2].wait_recv()
    rp[-2].wait_recv()
    rc.append(rput(x + 2, None, other))
    offs = {0: 0, 1: -1, -1: 1, 2: 2}
    for k in (1, -1, 2):
        for d in (1, -1):
            for h in range(2):
                p, s = pos[h]
                sec[h, k, d].wait_recv()
                sh[h, k, d] = cput(h, (p + offs[k], s - d), LO if d > 0 else HI, (p, s + d))
    for c in rc:
        c.wait_recv()
    for c in locals_:
        c.wait()

    lane = lax.broadcasted_iota(jnp.int32, (1, 128), 1)
    left = lane < 64

    def split_items(c, carry):
        col = pl.ds(pl.multiple_of(c * 128, 128), 128)
        v = rg[:, :, col].reshape(width, 128).T
        hi = v.astype(jnp.bfloat16)
        lo = (v - hi.astype(jnp.float32)).astype(jnp.bfloat16)
        for b in range(2):
            rt[2 * c + b, 0:64, :] = hi[b * 64 : b * 64 + 64]
            rt[2 * c + b, 64:128, :] = lo[b * 64 : b * 64 + 64]
        return carry

    lax.fori_loop(0, idv // 128, split_items, 0)

    for k in (0, 1, -1, 2):
        for d in (1, -1):
            for h in range(2):
                sh[h, k, d].wait_recv()

    def split_codes(q, carry):
        col = pl.ds(pl.multiple_of(q * 128, 128), 128)
        v = cg[:, :, :, col].reshape(width, 128)
        w = pltpu.roll(v, 64, 1)
        for b, t in ((0, v), (1, w)):
            hi = t.astype(jnp.bfloat16)
            vh[2 * q + b] = hi
            vl[2 * q + b] = (t - hi.astype(jnp.float32)).astype(jnp.bfloat16)
        return carry

    lax.fori_loop(0, cd // 128, split_codes, 0)

    lane64 = lax.broadcasted_iota(jnp.int32, (64, 128), 1)
    leftw = lax.broadcasted_iota(jnp.int32, (width, 128), 1) < 64

    def rows_at(k, b):
        return pl.ds(k * 64 + b, 1)

    def column(f, b):
        return jnp.sum(jnp.where(lane64 == b, f, 0.0), axis=1, keepdims=True)

    def score_block(b, acc):
        wh, wl = [], []
        for k in range(KP):
            i0 = ids_ref[b, 2 * k]
            i1 = ids_ref[b, 2 * k + 1]
            wh.append(jnp.where(leftw, vh[i0], vh[i1]))
            wl.append(jnp.where(leftw, vl[i0], vl[i1]))
        wh = jnp.concatenate(wh, axis=1)
        wl = jnp.concatenate(wl, axis=1)
        a = rt[b]
        d1 = jnp.dot(a, wh, preferred_element_type=jnp.float32)
        d2 = jnp.dot(a[0:64], wl, preferred_element_type=jnp.float32)
        s = (d1[0:64] + (d1[64:128] + d2)) * scale
        live = jnp.concatenate([tgt_ref[rows_at(k, b), :] for k in range(KP)], axis=1) >= 0
        s = jnp.where(live, s, NEG)
        s_ref[b] = s
        m = jnp.max(s, axis=1, keepdims=True)
        t = jnp.sum(jnp.exp(s - m), axis=1, keepdims=True)
        return jnp.where(lane64 == b, m + jnp.log(t), acc)

    row = lax.fori_loop(0, 64, score_block, jnp.zeros((64, 128), jnp.float32))

    lane32 = lax.broadcasted_iota(jnp.int32, (32, 128), 1) < 64

    def pack(r):
        return jnp.where(lane32, r[0:32], pltpu.roll(r[32:64], 64, 1))

    def unpack(m):
        return jnp.concatenate([m, pltpu.roll(m, 64, 1)], axis=0)

    def lse(parts):
        m = functools.reduce(jnp.maximum, parts)
        t = functools.reduce(jnp.add, [jnp.exp(q - m) for q in parts])
        return m + jnp.log(t)

    def total(parts):
        return functools.reduce(jnp.add, parts)

    def row_exchange(n, r, extra, merge):
        xrow[n, code, 0:32, :] = pack(r)
        size = 32
        if extra is not None:
            xrow[n, code, 32:40, :] = jnp.broadcast_to(extra, (8, 128))
            size = 40
        cs = []
        for d in range(1, 8):
            ref = xrow.at[n, code, pl.ds(0, size), :]
            i = n * 7 + d - 1
            cs.append(put(ref, ref, rowsend.at[i], rowrecv.at[i], ac((code + d) % 8)))
        for c in cs:
            c.wait_recv()
        out = unpack(merge([xrow[n, q, 0:32, :] for q in range(8)]))
        if extra is None:
            return out
        return out, total([xrow[n, q, 32:40, :] for q in range(8)])[0:1, 0:1]

    def one_axis(n, buf, me, ssem, rsem, dev, val, extra, merge):
        buf[n, me, 0:64, :] = val
        size = 64
        if extra is not None:
            buf[n, me, 64:72, :] = jnp.broadcast_to(extra, (8, 128))
            size = 72
        cs = []
        for d in range(1, 4):
            ref = buf.at[n, me, pl.ds(0, size), :]
            i = n * 3 + d - 1
            cs.append(put(ref, ref, ssem.at[i], rsem.at[i], dev(d)))
        for c in cs:
            c.wait_recv()
        out = merge([buf[n, q, 0:64, :] for q in range(4)])
        if extra is None:
            return out, None
        return out, total([buf[n, q, 64:72, :] for q in range(4)])[0:1, 0:1]

    def col_exchange(n, val, extra, merge):
        val, extra = one_axis(n, xy, y, ysend, yrecv, lambda d: at(z, y + d), val, extra, merge)
        return one_axis(n, xz, z, zsend, zrecv, lambda d: at(z + d, y), val, extra, merge)

    wt = wt_ref[...]
    cap = cap_ref[...]
    wsum = jnp.sum(jnp.where(lane64 < 64, wt, 0.0), keepdims=True)
    csum = jnp.sum(cap, keepdims=True)
    row, capacity = row_exchange(0, row, csum, lse)
    f1 = jnp.log(wt) - row

    def col_first(b, carry):
        c = s_ref[b] + column(f1, b)
        m = jnp.max(c, axis=0, keepdims=True)
        t = jnp.sum(jnp.exp(c - m), axis=0, keepdims=True)
        for k in range(KP):
            tm_ref[rows_at(k, b), :] = m[:, k * 128 : k * 128 + 128]
            ts_ref[rows_at(k, b), :] = t[:, k * 128 : k * 128 + 128]
        return carry

    lax.fori_loop(0, 64, col_first, 0)

    block = lax.broadcasted_iota(jnp.int32, (128, 128), 0)

    def spread_max(r, acc):
        for u in range(4):
            one = pl.ds(r * 4 + u, 1)
            acc = jnp.maximum(acc, jnp.where(block == tgt_ref[one, :], tm_ref[one, :], NEG))
        return acc

    peak = lax.fori_loop(0, 64, spread_max, jnp.full((128, 128), NEG, jnp.float32))
    peak = jnp.maximum(peak, pltpu.roll(peak, 64, 1))

    lanes = lax.broadcasted_iota(jnp.int32, (256, 128), 1)
    tgt = tgt_ref[...]
    hot_even = jnp.where(lanes == tgt[:, 0:1], 1.0, 0.0)
    hot_odd = jnp.where(lanes == tgt[:, 64:65], 1.0, 0.0)
    sub = lax.broadcasted_iota(jnp.int32, (128, 256), 0)
    hot_even_t = jnp.where(sub == tgtt_ref[0], 1.0, 0.0)
    hot_odd_t = jnp.where(sub == tgtt_ref[1], 1.0, 0.0)

    def dot(a, b):
        return jnp.dot(a, b, precision=HIGHEST, preferred_element_type=jnp.float32)

    def spread_out(v):
        return jnp.where(left, dot(hot_even, v), dot(hot_odd, v))

    def collect(v):
        o = dot(hot_even_t, jnp.where(left, v, 0.0)) + dot(hot_odd_t, jnp.where(left, 0.0, v))
        return o + pltpu.roll(o, 64, 1)

    def compact(v):
        return jnp.where(left, v[0:64], v[64:128])

    def expand(c):
        r = pltpu.roll(c, 64, 1)
        return jnp.concatenate([jnp.where(left, c, r), jnp.where(left, r, c)], axis=0)

    tiles = ts_ref[...] * jnp.exp(tm_ref[...] - spread_out(peak))
    sums = collect(tiles)
    some = sums > 0.0
    col = jnp.where(some, peak + jnp.log(jnp.where(some, sums, 1.0)), NEG)
    col, weight = col_exchange(0, compact(col), wsum, lse)
    lw = jnp.log(weight)
    f1 = f1 - lw
    g1 = jnp.log(cap) - jnp.log(capacity) - (col - lw)
    amass = wt / weight
    bmass = cap / capacity

    tm_ref[...] = spread_out(expand(g1))

    def first_rows(b, acc):
        g = jnp.concatenate([tm_ref[rows_at(k, b), :] for k in range(KP)], axis=1)
        e = jnp.exp(s_ref[b] + column(f1, b) + g)
        s_ref[b] = e
        return jnp.where(lane64 == b, jnp.sum(e, axis=1, keepdims=True), acc)

    row = lax.fori_loop(0, 64, first_rows, jnp.ones((64, 128), jnp.float32))
    u = amass / row_exchange(1, row, None, total)

    def cols(u):
        def body(b, carry):
            t = jnp.sum(s_ref[b] * column(u, b), axis=0, keepdims=True)
            for k in range(KP):
                ts_ref[rows_at(k, b), :] = t[:, k * 128 : k * 128 + 128]
            return carry

        lax.fori_loop(0, 64, body, 0)
        return compact(collect(ts_ref[...]))

    v = bmass / col_exchange(1, cols(u), None, total)[0]

    tm_ref[...] = spread_out(expand(v))

    def rows(b, acc):
        g = jnp.concatenate([tm_ref[rows_at(k, b), :] for k in range(KP)], axis=1)
        return jnp.where(lane64 == b, jnp.sum(s_ref[b] * g, axis=1, keepdims=True), acc)

    row = lax.fori_loop(0, 64, rows, jnp.ones((64, 128), jnp.float32))
    u = amass / row_exchange(2, row, None, total)
    fout_ref[...] = f1 + jnp.log(u)
    v = bmass / col_exchange(2, cols(u), None, total)[0]
    gout_ref[...] = g1 + jnp.log(v)

    for c in sends:
        c.wait_send()


def body(residuals, codebook, item_weight, code_capacity, pairs):
    items = residuals.shape[1]
    codes = codebook.shape[1]
    nb = items // BLOCK
    live = pairs >= 0
    slot = jnp.arange(pairs.shape[1], dtype=jnp.int32)
    rank = jnp.sum(live[:, None, :] & (slot[None, None, :] < slot[None, :, None]), axis=2)
    pick = live[:, None, :] & (rank[:, None, :] == jnp.arange(SLOTS, dtype=jnp.int32)[None, :, None])
    tgt = jnp.sum(jnp.where(pick, pairs[:, None, :] + 1, 0), axis=2) - 1
    flip = jnp.arange(SLOTS, dtype=jnp.int32) & 1
    ids = jnp.bitwise_xor(jnp.maximum(tgt, 0), flip[None, :])
    by_pair = tgt.T.reshape(KP, 2, nb)
    tgtt = by_pair.transpose(1, 0, 2).reshape(2, 1, KP * nb)
    tgtrow = jnp.repeat(by_pair.transpose(0, 2, 1).reshape(KP * nb, 2), 64, axis=1)
    wt = jnp.pad(item_weight.reshape(nb, BLOCK).T, ((0, 0), (0, 128 - nb)), constant_values=1.0)
    cap = code_capacity.reshape(2, 64, BLOCK).transpose(1, 0, 2).reshape(64, 128)
    vm = pl.BlockSpec(memory_space=pltpu.VMEM)
    hbm = pl.BlockSpec(memory_space=pl.ANY)
    f32, bf16 = jnp.float32, jnp.bfloat16
    dma = pltpu.SemaphoreType.DMA
    f, g = pl.pallas_call(
        kernel,
        out_shape=[jax.ShapeDtypeStruct((64, 128), f32), jax.ShapeDtypeStruct((64, 128), f32)],
        in_specs=[hbm, hbm, vm, vm, vm, vm, pl.BlockSpec(memory_space=pltpu.SMEM)],
        out_specs=[vm, vm],
        scratch_shapes=[
            pltpu.VMEM((16, 2, 8, codes), f32),
            pltpu.VMEM((8, 32, items), f32),
            pltpu.VMEM((128, 256, 128), bf16),
            pltpu.VMEM((128, 256, 128), bf16),
            pltpu.VMEM((64, 128, 256), bf16),
            pltpu.VMEM((64, 64, 512), f32),
            pltpu.VMEM((256, 128), f32),
            pltpu.VMEM((256, 128), f32),
            pltpu.VMEM((3, 8, 40, 128), f32),
            pltpu.VMEM((3, 4, 72, 128), f32),
            pltpu.VMEM((3, 4, 72, 128), f32),
            dma((40,)),
            dma((40,)),
            dma((8,)),
            dma((8,)),
            dma((3,)),
            dma((21,)),
            dma((21,)),
            dma((9,)),
            dma((9,)),
            dma((9,)),
            dma((9,)),
        ],
        compiler_params=pltpu.CompilerParams(
            collective_id=0, has_side_effects=True, vmem_limit_bytes=60 * 1024 * 1024
        ),
    )(codebook.reshape(2, 8, codes), residuals, wt, cap, tgtrow, tgtt, ids)
    f = f[:, :nb].T.reshape(items)
    g = g.reshape(64, 2, BLOCK).transpose(1, 0, 2).reshape(codes)
    return f, g


def solution(mesh):
    placed = (P("code", "item"), P("item", "code"), P("item"), P("code"), P("item", "code"))
    return jax.shard_map(
        body, mesh=mesh, in_specs=placed, out_specs=(P("item"), P("code")), check_vma=False
    )
```

```python
import functools
import math

import jax
import jax.numpy as jnp
from jax import lax
from jax.experimental import pallas as pl
from jax.experimental.pallas import tpu as pltpu
from jax.sharding import PartitionSpec as P

BLOCK = 64
SLOTS = 8
KP = SLOTS // 2
NEG = -1e30
SOFTNESS = 0.1
MESH = pl.DeviceIdType.MESH


def kernel(
    cb_ref,
    res_ref,
    wt_ref,
    cap_ref,
    pairs_ref,
    fout_ref,
    gout_ref,
    cg,
    rg,
    vh,
    vl,
    rt,
    s_ref,
    padded,
    tgt_ref,
    ids_v,
    ids_ref,
    tm_ref,
    ts_ref,
    xrow,
    xy,
    xz,
    csend,
    crecv,
    rsend,
    rrecv,
    lsem,
    rowsend,
    rowrecv,
    ysend,
    yrecv,
    zsend,
    zrecv,
):
    item = lax.axis_index("item")
    code = lax.axis_index("code")
    z, y = item // 4, item % 4
    x, core = code // 2, code % 2
    cd = cg.shape[3]
    idv = rg.shape[2]
    width = 256
    scale = 1.0 / (SOFTNESS * math.sqrt(width))

    def at(zz, yy):
        return {"item": (zz % 4) * 4 + yy % 4, "code": code}

    def ac(cc):
        return {"item": item, "code": cc}

    bar = pltpu.get_barrier_semaphore()
    for d in range(1, 4):
        pl.semaphore_signal(bar, inc=1, device_id=at(z, y + d), device_id_type=MESH)
        pl.semaphore_signal(bar, inc=1, device_id=at(z + d, y), device_id_type=MESH)
    for d in range(1, 8):
        pl.semaphore_signal(bar, inc=1, device_id=ac((code + d) % 8), device_id_type=MESH)

    lane = lax.broadcasted_iota(jnp.int32, (1, 128), 1)
    left = lane < 64
    lane64 = lax.broadcasted_iota(jnp.int32, (64, 128), 1)
    padded[...] = jnp.full((64, 128), -1, jnp.int32)
    padded[:, 0:16] = pairs_ref[...]
    named = padded[...]
    live = jnp.where(named >= 0, 1, 0)
    count = live
    for sh in (1, 2, 4, 8):
        count = count + jnp.where(lane64 >= sh, pltpu.roll(count, sh, 1), 0)
    count = live * count
    picked = []
    ids = jnp.zeros((64, 128), jnp.int32)
    for k in range(SLOTS):
        one = jnp.max(jnp.where(count == k + 1, named, -1), axis=1, keepdims=True)
        ids = jnp.where(lane64 == k, jnp.maximum(one, 0) ^ (k & 1), ids)
        picked.append(jnp.where(one < 0, -1, (one >> 1) + (one & 1) * 64))
    for k in range(KP):
        tgt_ref[k * 64 : k * 64 + 64, :] = jnp.where(left, picked[2 * k], picked[2 * k + 1])
    ids_v[...] = ids
    idc = pltpu.make_async_copy(ids_v, ids_ref, lsem.at[3])
    idc.start()
    idc.wait()
    pl.semaphore_wait(bar, 13)

    half = cd // 2
    LO, HI = slice(0, half), slice(half, cd)
    sends = []

    def put(src, dst, ss, rs, dev):
        c = pltpu.make_async_remote_copy(
            src_ref=src, dst_ref=dst, send_sem=ss, recv_sem=rs, device_id=dev, device_id_type=MESH
        )
        c.start()
        sends.append(c)
        return c

    def place(h, p, s):
        zz, yy = (s, p) if h == 0 else (p, s)
        return (zz % 4) * 4 + yy % 4

    def where_to(h, p, s):
        zz, yy = (s, p) if h == 0 else (p, s)
        return at(zz, yy)

    pos = [(y, z), (z, y)]
    cnt = [0]

    def piece(h, p, s, cols=None, own=False):
        if own:
            return cb_ref.at[h]
        d = place(h, p, s)
        if cols is None:
            return cg.at[d, h]
        return cg.at[d, h, :, pl.ds(cols.start, cols.stop - cols.start)]

    def cput(h, src_ps, cols, to, own=False):
        i = cnt[0]
        cnt[0] += 1
        src = piece(h, *src_ps, cols, own)
        dst = piece(h, *src_ps, cols)
        return put(src, dst, csend.at[i], crecv.at[i], where_to(h, *to))

    prim, sec = {}, {}
    locals_ = []
    for h in range(2):
        p, s = pos[h]
        prim[h, 1] = cput(h, (p, s), None, (p + 1, s), True)
        prim[h, -1] = cput(h, (p, s), None, (p - 1, s), True)
        sec[h, 0, 1] = cput(h, (p, s), None, (p, s + 1), True)
        sec[h, 0, -1] = cput(h, (p, s), None, (p, s - 1), True)
        lc = pltpu.make_async_copy(cb_ref.at[h], cg.at[item, h], lsem.at[h])
        lc.start()
        locals_.append(lc)

    rhalf = idv // 2
    rcnt = [0]

    def rdev(xx):
        return (xx % 4) * 2 + core

    def rput(xx, cols, to, own=False):
        i = rcnt[0]
        rcnt[0] += 1
        d = rdev(xx)
        if cols is None:
            dst = rg.at[d]
        else:
            dst = rg.at[d, :, pl.ds(cols * rhalf, rhalf)]
        return put(res_ref if own else dst, dst, rsend.at[i], rrecv.at[i], ac(to))

    other = x * 2 + (1 - core)
    rp = {}
    rp[1] = rput(x, None, rdev(x + 1), True)
    rp[-1] = rput(x, None, rdev(x - 1), True)
    rc = [rput(x, None, other, True)]
    lc = pltpu.make_async_copy(res_ref, rg.at[code], lsem.at[2])
    lc.start()
    locals_.append(lc)

    tasks = []
    parts = {}

    def split_items(c, carry):
        col = pl.ds(pl.multiple_of(c * 128, 128), 128)
        v = rg[:, :, col].reshape(width, 128).T * scale
        hi = v.astype(jnp.bfloat16)
        lo = (v - hi.astype(jnp.float32)).astype(jnp.bfloat16)
        for b in range(2):
            rt[2 * c + b, 0:64, :] = hi[b * 64 : b * 64 + 64]
            rt[2 * c + b, 64:128, :] = lo[b * 64 : b * 64 + 64]
        return carry

    def split_codes(d):
        def step(j, carry):
            for r in range(8):
                q = j * 8 + r
                col = pl.ds(pl.multiple_of(q * 128, 128), 128)
                v = cg[d, :, :, col].reshape(16, 128)
                for b, t in ((0, v), (1, pltpu.roll(v, 64, 1))):
                    hi = t.astype(jnp.bfloat16)
                    vh[2 * q + b, d] = hi
                    vl[2 * q + b, d] = (t - hi.astype(jnp.float32)).astype(jnp.bfloat16)
            return carry

        lax.fori_loop(0, cd // 1024, step, 0)

    def got(h, op, os, share):
        dy, dz = ((op, os) if h == 0 else (os, op))
        key = dy % 4, dz % 4
        parts[key] = parts.get(key, 0) + share
        if parts[key] == 4:
            d = ((z + dz) % 4) * 4 + (y + dy) % 4
            tasks.append(lambda: split_codes(d))

    def work(n):
        for _ in range(min(n, len(tasks))):
            tasks.pop(0)()

    ph, sh = {}, {}
    for d in (1, -1):
        for h in range(2):
            p, s = pos[h]
            prim[h, d].wait_recv()
            got(h, -d, 0, 2)
            ph[h, d] = cput(h, (p - d, s), LO if d > 0 else HI, (p + d, s))
            sec[h, d, 1] = cput(h, (p - d, s), None, (p, s + 1))
            sec[h, d, -1] = cput(h, (p - d, s), None, (p, s - 1))
        rp[d].wait_recv()
        rp[2 * d] = rput(x - d, 0 if d > 0 else 1, rdev(x + d))
        rc.append(rput(x - d, None, other))
        for h in range(2):
            p, s = pos[h]
            sec[h, 0, d].wait_recv()
            got(h, 0, -d, 2)
            sh[h, 0, d] = cput(h, (p, s - d), LO if d > 0 else HI, (p, s + d))
    for c in locals_:
        c.wait()
    for h in range(2):
        got(h, 0, 0, 2)
    for h in range(2):
        p, s = pos[h]
        work(1)
        ph[h, 1].wait_recv()
        ph[h, -1].wait_recv()
        got(h, 2, 0, 2)
        sec[h, 2, 1] = cput(h, (p + 2, s), None, (p, s + 1))
        sec[h, 2, -1] = cput(h, (p + 2, s), None, (p, s - 1))
    rp[2].wait_recv()
    rp[-2].wait_recv()
    rc.append(rput(x + 2, None, other))
    offs = {0: 0, 1: -1, -1: 1, 2: 2}

    def secondary(k):
        for d in (1, -1):
            for h in range(2):
                p, s = pos[h]
                work(1)
                sec[h, k, d].wait_recv()
                got(h, offs[k], -d, 2)
                sh[h, k, d] = cput(h, (p + offs[k], s - d), LO if d > 0 else HI, (p, s + d))

    def halves(k):
        for d in (1, -1):
            for h in range(2):
                work(1)
                sh[h, k, d].wait_recv()
                got(h, offs[k], 2, 1)

    secondary(1)
    for c in rc:
        c.wait_recv()
    for g in range(8):
        n = idv // 128 // 8
        tasks.append(lambda g=g, n=n: lax.fori_loop(g * n, g * n + n, split_items, 0))
    secondary(-1)
    halves(0)
    secondary(2)
    for k in (1, -1, 2):
        halves(k)
    work(len(tasks))

    UN = 4

    def rows_at(k, b):
        return pl.ds(k * 64 + b, 1)

    def home(b):
        return (b & 1) * 32 + (b >> 1)

    def column(f, b):
        return jnp.sum(jnp.where(lane64 == home(b), f, 0.0), axis=1, keepdims=True)

    def ks(k):
        return slice(k * 128, k * 128 + 128)

    def blocks(body, init, un=UN):
        def step(j, acc):
            for r in range(un):
                acc = body(j * un + r, acc)
            return acc

        return lax.fori_loop(0, 64 // un, step, init)

    def score_block(b, acc):
        a = rt[b]
        ss = []
        for k in range(KP):
            i0 = ids_ref[b, 2 * k]
            i1 = ids_ref[b, 2 * k + 1]
            wh = jnp.concatenate([vh[i0].reshape(width, 128), vh[i1].reshape(width, 128)], axis=1)
            wl = jnp.concatenate([vl[i0].reshape(width, 128), vl[i1].reshape(width, 128)], axis=1)
            d1 = jnp.dot(a, wh, preferred_element_type=jnp.float32)
            d2 = jnp.dot(a[0:64], wl, preferred_element_type=jnp.float32)
            t = d1[0:64] + (d1[64:128] + d2)
            s = jnp.where(left, t[:, 0:128], t[:, 128:256])
            s = jnp.where(tgt_ref[rows_at(k, b), :] >= 0, s, NEG)
            s_ref[b, :, ks(k)] = s
            ss.append(s)
        m = jnp.max(functools.reduce(jnp.maximum, ss), axis=1, keepdims=True)
        t = functools.reduce(jnp.add, [jnp.exp(s - m) for s in ss])
        t = jnp.sum(t, axis=1, keepdims=True)
        return jnp.where(lane64 == home(b), m + jnp.log(t), acc)

    row = blocks(score_block, jnp.zeros((64, 128), jnp.float32), 2)

    lane32 = lax.broadcasted_iota(jnp.int32, (32, 128), 1) < 64

    def pack(r):
        return jnp.where(lane32, r[0:32], pltpu.roll(r[32:64], 64, 1))

    def unpack(m):
        return jnp.concatenate([m, pltpu.roll(m, 64, 1)], axis=0)

    def lse(parts):
        m = functools.reduce(jnp.maximum, parts)
        t = functools.reduce(jnp.add, [jnp.exp(q - m) for q in parts])
        return m + jnp.log(t)

    def total(parts):
        return functools.reduce(jnp.add, parts)

    def row_exchange(n, r, extra, merge):
        xrow[n, code, 0:32, :] = pack(r)
        size = 32
        if extra is not None:
            xrow[n, code, 32:40, :] = jnp.broadcast_to(extra, (8, 128))
            size = 40
        cs = []
        for d in range(1, 8):
            ref = xrow.at[n, code, pl.ds(0, size), :]
            i = n * 7 + d - 1
            cs.append(put(ref, ref, rowsend.at[i], rowrecv.at[i], ac((code + d) % 8)))
        for c in cs:
            c.wait_recv()
        out = unpack(merge([xrow[n, q, 0:32, :] for q in range(8)]))
        if extra is None:
            return out
        return out, total([xrow[n, q, 32:40, :] for q in range(8)])[0:1, 0:1]

    def one_axis(n, buf, me, ssem, rsem, dev, val, extra, merge):
        buf[n, me, 0:64, :] = val
        size = 64
        if extra is not None:
            buf[n, me, 64:72, :] = jnp.broadcast_to(extra, (8, 128))
            size = 72
        cs = []
        for d in range(1, 4):
            ref = buf.at[n, me, pl.ds(0, size), :]
            i = n * 3 + d - 1
            cs.append(put(ref, ref, ssem.at[i], rsem.at[i], dev(d)))
        for c in cs:
            c.wait_recv()
        out = merge([buf[n, q, 0:64, :] for q in range(4)])
        if extra is None:
            return out, None
        return out, total([buf[n, q, 64:72, :] for q in range(4)])[0:1, 0:1]

    def col_exchange(n, val, extra, merge):
        val, extra = one_axis(n, xy, y, ysend, yrecv, lambda d: at(z, y + d), val, extra, merge)
        return one_axis(n, xz, z, zsend, zrecv, lambda d: at(z + d, y), val, extra, merge)

    turned = jnp.concatenate([wt_ref[...], jnp.ones((96, 128), jnp.float32)], axis=0).T
    wt = jnp.where(lane64 < 32, turned[0:64], pltpu.roll(turned[64:128], 32, 1))
    cap = cap_ref[...]
    wsum = jnp.sum(jnp.where(lane64 < 64, wt, 0.0), keepdims=True)
    csum = jnp.sum(cap, keepdims=True)
    row, capacity = row_exchange(0, row, csum, lse)
    f1 = jnp.log(wt) - row

    def col_first(b, carry):
        f = column(f1, b)
        for k in range(KP):
            c = s_ref[b, :, ks(k)] + f
            m = jnp.max(c, axis=0, keepdims=True)
            tm_ref[rows_at(k, b), :] = m
            ts_ref[rows_at(k, b), :] = jnp.sum(jnp.exp(c - m), axis=0, keepdims=True)
        return carry

    blocks(col_first, 0)

    block = lax.broadcasted_iota(jnp.int32, (128, 128), 0)

    def spread_max(r, acc):
        for u in range(4):
            one = pl.ds(r * 4 + u, 1)
            acc = jnp.maximum(acc, jnp.where(block == tgt_ref[one, :], tm_ref[one, :], NEG))
        return acc

    peak = lax.fori_loop(0, 64, spread_max, jnp.full((128, 128), NEG, jnp.float32))
    peak = jnp.maximum(peak, pltpu.roll(peak, 64, 1))

    lanes = lax.broadcasted_iota(jnp.int32, (256, 128), 1)
    tgt = tgt_ref[...]
    hot = jnp.concatenate(
        [jnp.where(lanes == tgt[:, 0:1], 1.0, 0.0), jnp.where(lanes == tgt[:, 64:65], 1.0, 0.0)], axis=1
    )
    hot_t = jnp.concatenate(
        [hot[:, 0:128].T, hot[:, 128:256].T], axis=1
    ).astype(jnp.bfloat16)
    hot = hot.astype(jnp.bfloat16)

    def hot_dot(one, v):
        out = []
        for _ in range(3):
            h = v.astype(jnp.bfloat16).astype(jnp.float32)
            out.append(h)
            v = v - h
        w = jnp.concatenate(out, axis=1)
        side = (lax.broadcasted_iota(jnp.int32, (1, 384), 1) & 64) == 0
        w = jnp.concatenate([jnp.where(side, w, 0.0), jnp.where(side, 0.0, w)], axis=0)
        o = jnp.dot(one, w.astype(jnp.bfloat16), preferred_element_type=jnp.float32)
        return o[:, 0:128] + (o[:, 128:256] + o[:, 256:384])

    def spread_out(v):
        return hot_dot(hot, v)

    def collect(v):
        o = hot_dot(hot_t, v)
        return o + pltpu.roll(o, 64, 1)

    def compact(v):
        return jnp.where(left, v[0:64], v[64:128])

    def expand(c):
        r = pltpu.roll(c, 64, 1)
        return jnp.concatenate([jnp.where(left, c, r), jnp.where(left, r, c)], axis=0)

    tiles = ts_ref[...] * jnp.exp(tm_ref[...] - spread_out(peak))
    sums = collect(tiles)
    some = sums > 0.0
    col = jnp.where(some, peak + jnp.log(jnp.where(some, sums, 1.0)), NEG)
    col, weight = col_exchange(0, compact(col), wsum, lse)
    lw = jnp.log(weight)
    f1 = f1 - lw
    g1 = jnp.log(cap) - jnp.log(capacity) - (col - lw)
    amass = wt / weight
    bmass = cap / capacity

    tm_ref[...] = spread_out(expand(g1))

    def first_rows(b, acc):
        f = column(f1, b)
        t = None
        for k in range(KP):
            e = jnp.exp(s_ref[b, :, ks(k)] + f + tm_ref[rows_at(k, b), :])
            s_ref[b, :, ks(k)] = e
            t = e if t is None else t + e
        return jnp.where(lane64 == home(b), jnp.sum(t, axis=1, keepdims=True), acc)

    row = blocks(first_rows, jnp.ones((64, 128), jnp.float32))
    u = amass / row_exchange(1, row, None, total)

    def cols(u):
        def body(b, carry):
            c = column(u, b)
            for k in range(KP):
                ts_ref[rows_at(k, b), :] = jnp.sum(s_ref[b, :, ks(k)] * c, axis=0, keepdims=True)
            return carry

        blocks(body, 0)
        return compact(collect(ts_ref[...]))

    v = bmass / col_exchange(1, cols(u), None, total)[0]

    tm_ref[...] = spread_out(expand(v))

    def rows(b, acc):
        t = functools.reduce(
            jnp.add, [s_ref[b, :, ks(k)] * tm_ref[rows_at(k, b), :] for k in range(KP)]
        )
        return jnp.where(lane64 == home(b), jnp.sum(t, axis=1, keepdims=True), acc)

    row = blocks(rows, jnp.ones((64, 128), jnp.float32))
    u = amass / row_exchange(2, row, None, total)
    f = f1 + jnp.log(u)
    fout_ref[...] = jnp.concatenate([f, pltpu.roll(f, 96, 1)], axis=0).T[0:32]
    v = bmass / col_exchange(2, cols(u), None, total)[0]
    gout_ref[...] = g1 + jnp.log(v)

    for c in sends:
        c.wait_send()


def body(residuals, codebook, item_weight, code_capacity, pairs):
    items = residuals.shape[1]
    codes = codebook.shape[1]
    vm = pl.BlockSpec(memory_space=pltpu.VMEM)
    hbm = pl.BlockSpec(memory_space=pl.ANY)
    f32, bf16 = jnp.float32, jnp.bfloat16
    dma = pltpu.SemaphoreType.DMA
    f, g = pl.pallas_call(
        kernel,
        out_shape=[jax.ShapeDtypeStruct((32, 128), f32), jax.ShapeDtypeStruct((64, 128), f32)],
        in_specs=[hbm, hbm, vm, vm, vm],
        out_specs=[vm, vm],
        scratch_shapes=[
            pltpu.VMEM((16, 2, 8, codes), f32),
            pltpu.VMEM((8, 32, items), f32),
            pltpu.VMEM((128, 16, 16, 128), bf16),
            pltpu.VMEM((128, 16, 16, 128), bf16),
            pltpu.VMEM((64, 128, 256), bf16),
            pltpu.VMEM((64, 64, 512), f32),
            pltpu.VMEM((64, 128), jnp.int32),
            pltpu.VMEM((256, 128), jnp.int32),
            pltpu.VMEM((64, 128), jnp.int32),
            pltpu.SMEM((64, 128), jnp.int32),
            pltpu.VMEM((256, 128), f32),
            pltpu.VMEM((256, 128), f32),
            pltpu.VMEM((3, 8, 40, 128), f32),
            pltpu.VMEM((3, 4, 72, 128), f32),
            pltpu.VMEM((3, 4, 72, 128), f32),
            dma((40,)),
            dma((40,)),
            dma((8,)),
            dma((8,)),
            dma((4,)),
            dma((21,)),
            dma((21,)),
            dma((9,)),
            dma((9,)),
            dma((9,)),
            dma((9,)),
        ],
        compiler_params=pltpu.CompilerParams(
            collective_id=0, has_side_effects=True, vmem_limit_bytes=60 * 1024 * 1024
        ),
    )(
        codebook.reshape(2, 8, codes),
        residuals,
        item_weight.reshape(32, 128),
        code_capacity.reshape(64, 128),
        pairs,
    )
    return f.reshape(items), g.reshape(codes)


def solution(mesh):
    placed = (P("code", "item"), P("item", "code"), P("item"), P("code"), P("item", "code"))
    return jax.shard_map(
        body, mesh=mesh, in_specs=placed, out_specs=(P("item"), P("code")), check_vma=False
    )
```

```python
import functools
import math

import jax
import jax.numpy as jnp
from jax import lax
from jax.experimental import pallas as pl
from jax.experimental.pallas import tpu as pltpu
from jax.sharding import PartitionSpec as P

BLOCK = 64
SLOTS = 8
KP = SLOTS // 2
NEG = -1e30
SOFTNESS = 0.1
MESH = pl.DeviceIdType.MESH


def kernel(
    cb_ref,
    res_ref,
    wt_ref,
    cap_ref,
    pairs_ref,
    fout_ref,
    gout_ref,
    cg,
    rg,
    vh,
    vl,
    rt,
    s_ref,
    padded,
    tgt_ref,
    ids_v,
    ids_ref,
    tm_ref,
    ts_ref,
    xrow,
    xy,
    xz,
    csend,
    crecv,
    rsend,
    rrecv,
    lsem,
    rowsend,
    rowrecv,
    ysend,
    yrecv,
    zsend,
    zrecv,
):
    item = lax.axis_index("item")
    code = lax.axis_index("code")
    z, y = item // 4, item % 4
    x, core = code // 2, code % 2
    cd = cg.shape[3]
    idv = rg.shape[2]
    width = 256
    scale = 1.0 / (SOFTNESS * math.sqrt(width))

    def at(zz, yy):
        return {"item": (zz % 4) * 4 + yy % 4, "code": code}

    def ac(cc):
        return {"item": item, "code": cc}

    bar = pltpu.get_barrier_semaphore()
    for d in range(1, 4):
        pl.semaphore_signal(bar, inc=1, device_id=at(z, y + d), device_id_type=MESH)
        pl.semaphore_signal(bar, inc=1, device_id=at(z + d, y), device_id_type=MESH)
    for d in range(1, 8):
        pl.semaphore_signal(bar, inc=1, device_id=ac((code + d) % 8), device_id_type=MESH)

    lane = lax.broadcasted_iota(jnp.int32, (1, 128), 1)
    left = lane < 64
    lane64 = lax.broadcasted_iota(jnp.int32, (64, 128), 1)
    padded[...] = jnp.full((64, 128), -1, jnp.int32)
    padded[:, 0:16] = pairs_ref[...]
    named = padded[...]
    live = jnp.where(named >= 0, 1, 0)
    count = live
    for sh in (1, 2, 4, 8):
        count = count + jnp.where(lane64 >= sh, pltpu.roll(count, sh, 1), 0)
    count = live * count
    picked = []
    ids = jnp.zeros((64, 128), jnp.int32)
    for k in range(SLOTS):
        one = jnp.max(jnp.where(count == k + 1, named, -1), axis=1, keepdims=True)
        ids = jnp.where(lane64 == k, jnp.maximum(one, 0) ^ (k & 1), ids)
        picked.append(jnp.where(one < 0, -1, (one >> 1) + (one & 1) * 64))
    for k in range(KP):
        tgt_ref[k * 64 : k * 64 + 64, :] = jnp.where(left, picked[2 * k], picked[2 * k + 1])
    ids_v[...] = ids
    idc = pltpu.make_async_copy(ids_v, ids_ref, lsem.at[3])
    idc.start()
    idc.wait()
    pl.semaphore_wait(bar, 13)

    half = cd // 2
    LO, HI = slice(0, half), slice(half, cd)
    sends = []

    def put(src, dst, ss, rs, dev):
        c = pltpu.make_async_remote_copy(
            src_ref=src, dst_ref=dst, send_sem=ss, recv_sem=rs, device_id=dev, device_id_type=MESH
        )
        c.start()
        sends.append(c)
        return c

    def place(h, p, s):
        zz, yy = (s, p) if h == 0 else (p, s)
        return (zz % 4) * 4 + yy % 4

    def where_to(h, p, s):
        zz, yy = (s, p) if h == 0 else (p, s)
        return at(zz, yy)

    pos = [(y, z), (z, y)]
    cnt = [0]

    def piece(h, p, s, cols=None, own=False):
        if own:
            return cb_ref.at[h]
        d = place(h, p, s)
        if cols is None:
            return cg.at[d, h]
        return cg.at[d, h, :, pl.ds(cols.start, cols.stop - cols.start)]

    def cput(h, src_ps, cols, to, own=False):
        i = cnt[0]
        cnt[0] += 1
        src = piece(h, *src_ps, cols, own)
        dst = piece(h, *src_ps, cols)
        return put(src, dst, csend.at[i], crecv.at[i], where_to(h, *to))

    prim, sec = {}, {}
    locals_ = []
    for h in range(2):
        p, s = pos[h]
        prim[h, 1] = cput(h, (p, s), None, (p + 1, s), True)
        prim[h, -1] = cput(h, (p, s), None, (p - 1, s), True)
        sec[h, 0, 1] = cput(h, (p, s), None, (p, s + 1), True)
        sec[h, 0, -1] = cput(h, (p, s), None, (p, s - 1), True)
        lc = pltpu.make_async_copy(cb_ref.at[h], cg.at[item, h], lsem.at[h])
        lc.start()
        locals_.append(lc)

    rhalf = idv // 2
    rcnt = [0]

    def rdev(xx):
        return (xx % 4) * 2 + core

    def rput(xx, cols, to, own=False):
        i = rcnt[0]
        rcnt[0] += 1
        d = rdev(xx)
        if cols is None:
            dst = rg.at[d]
        else:
            dst = rg.at[d, :, pl.ds(cols * rhalf, rhalf)]
        return put(res_ref if own else dst, dst, rsend.at[i], rrecv.at[i], ac(to))

    other = x * 2 + (1 - core)
    rp = {}
    rp[1] = rput(x, None, rdev(x + 1), True)
    rp[-1] = rput(x, None, rdev(x - 1), True)
    rc = [rput(x, None, other, True)]
    lc = pltpu.make_async_copy(res_ref, rg.at[code], lsem.at[2])
    lc.start()
    locals_.append(lc)

    tasks = []
    parts = {}

    def split_items(c, carry):
        col = pl.ds(pl.multiple_of(c * 128, 128), 128)
        v = rg[:, :, col].reshape(width, 128).T * scale
        hi = v.astype(jnp.bfloat16)
        lo = (v - hi.astype(jnp.float32)).astype(jnp.bfloat16)
        for b in range(2):
            rt[2 * c + b, 0:64, :] = hi[b * 64 : b * 64 + 64]
            rt[2 * c + b, 64:128, :] = lo[b * 64 : b * 64 + 64]
        return carry

    def split_codes(d):
        def step(j, carry):
            for r in range(8):
                q = j * 8 + r
                col = pl.ds(pl.multiple_of(q * 128, 128), 128)
                v = cg[d, :, :, col].reshape(16, 128)
                for b, t in ((0, v), (1, pltpu.roll(v, 64, 1))):
                    hi = t.astype(jnp.bfloat16)
                    vh[2 * q + b, d] = hi
                    vl[2 * q + b, d] = (t - hi.astype(jnp.float32)).astype(jnp.bfloat16)
            return carry

        lax.fori_loop(0, cd // 1024, step, 0)

    def got(h, op, os, share):
        dy, dz = ((op, os) if h == 0 else (os, op))
        key = dy % 4, dz % 4
        parts[key] = parts.get(key, 0) + share
        if parts[key] == 4:
            d = ((z + dz) % 4) * 4 + (y + dy) % 4
            tasks.append(lambda: split_codes(d))

    def work(n):
        for _ in range(min(n, len(tasks))):
            tasks.pop(0)()

    ph, sh = {}, {}
    for d in (1, -1):
        for h in range(2):
            p, s = pos[h]
            prim[h, d].wait_recv()
            got(h, -d, 0, 2)
            ph[h, d] = cput(h, (p - d, s), LO if d > 0 else HI, (p + d, s))
            sec[h, d, 1] = cput(h, (p - d, s), None, (p, s + 1))
            sec[h, d, -1] = cput(h, (p - d, s), None, (p, s - 1))
        rp[d].wait_recv()
        rp[2 * d] = rput(x - d, 0 if d > 0 else 1, rdev(x + d))
        rc.append(rput(x - d, None, other))
        for h in range(2):
            p, s = pos[h]
            sec[h, 0, d].wait_recv()
            got(h, 0, -d, 2)
            sh[h, 0, d] = cput(h, (p, s - d), LO if d > 0 else HI, (p, s + d))
    for c in locals_:
        c.wait()
    for h in range(2):
        got(h, 0, 0, 2)
    for h in range(2):
        p, s = pos[h]
        work(1)
        ph[h, 1].wait_recv()
        ph[h, -1].wait_recv()
        got(h, 2, 0, 2)
        sec[h, 2, 1] = cput(h, (p + 2, s), None, (p, s + 1))
        sec[h, 2, -1] = cput(h, (p + 2, s), None, (p, s - 1))
    rp[2].wait_recv()
    rp[-2].wait_recv()
    rc.append(rput(x + 2, None, other))
    offs = {0: 0, 1: -1, -1: 1, 2: 2}

    def secondary(k):
        for d in (1, -1):
            for h in range(2):
                p, s = pos[h]
                work(1)
                sec[h, k, d].wait_recv()
                got(h, offs[k], -d, 2)
                sh[h, k, d] = cput(h, (p + offs[k], s - d), LO if d > 0 else HI, (p, s + d))

    def halves(k):
        for d in (1, -1):
            for h in range(2):
                work(1)
                sh[h, k, d].wait_recv()
                got(h, offs[k], 2, 1)

    secondary(1)
    for c in rc:
        c.wait_recv()
    for g in range(8):
        n = idv // 128 // 8
        tasks.append(lambda g=g, n=n: lax.fori_loop(g * n, g * n + n, split_items, 0))
    secondary(-1)
    halves(0)
    secondary(2)
    for k in (1, -1, 2):
        halves(k)
    work(len(tasks))

    UN = 8
    leftw = lax.broadcasted_iota(jnp.int32, (width, 128), 1) < 64

    def rows_at(k, b):
        return pl.ds(k * 64 + b, 1)

    def home(b):
        return (b & 1) * 32 + (b >> 1)

    def column(f, b):
        return jnp.sum(jnp.where(lane64 == home(b), f, 0.0), axis=1, keepdims=True)

    def ks(k):
        return slice(k * 128, k * 128 + 128)

    def blocks(body, init, un=UN):
        def step(j, acc):
            for r in range(un):
                acc = body(j * un + r, acc)
            return acc

        return lax.fori_loop(0, 64 // un, step, init)

    def score_block(b, acc):
        a = rt[b]
        wh, wl = [], []
        for k in range(KP):
            i0 = ids_ref[b, 2 * k]
            i1 = ids_ref[b, 2 * k + 1]
            wh.append(jnp.where(leftw, vh[i0].reshape(width, 128), vh[i1].reshape(width, 128)))
            wl.append(jnp.where(leftw, vl[i0].reshape(width, 128), vl[i1].reshape(width, 128)))
        ss = []
        for k in range(0, KP, 2):
            d1 = jnp.dot(a, jnp.concatenate(wh[k : k + 2], axis=1), preferred_element_type=jnp.float32)
            d2 = jnp.dot(
                a[0:64], jnp.concatenate(wl[k : k + 2], axis=1), preferred_element_type=jnp.float32
            )
            t = d1[0:64] + (d1[64:128] + d2)
            ss += [t[:, 0:128], t[:, 128:256]]
        for k in range(KP):
            ss[k] = jnp.where(tgt_ref[rows_at(k, b), :] >= 0, ss[k], NEG)
            s_ref[b, :, ks(k)] = ss[k]
        m = jnp.max(functools.reduce(jnp.maximum, ss), axis=1, keepdims=True)
        t = functools.reduce(jnp.add, [jnp.exp(s - m) for s in ss])
        t = jnp.sum(t, axis=1, keepdims=True)
        return jnp.where(lane64 == home(b), m + jnp.log(t), acc)

    row = blocks(score_block, jnp.zeros((64, 128), jnp.float32), 8)

    lane32 = lax.broadcasted_iota(jnp.int32, (32, 128), 1) < 64

    def pack(r):
        return jnp.where(lane32, r[0:32], pltpu.roll(r[32:64], 64, 1))

    def unpack(m):
        return jnp.concatenate([m, pltpu.roll(m, 64, 1)], axis=0)

    def lse(parts):
        m = functools.reduce(jnp.maximum, parts)
        t = functools.reduce(jnp.add, [jnp.exp(q - m) for q in parts])
        return m + jnp.log(t)

    def total(parts):
        return functools.reduce(jnp.add, parts)

    def row_exchange(n, r, extra, merge):
        xrow[n, code, 0:32, :] = pack(r)
        size = 32
        if extra is not None:
            xrow[n, code, 32:40, :] = jnp.broadcast_to(extra, (8, 128))
            size = 40
        cs = []
        for d in range(1, 8):
            ref = xrow.at[n, code, pl.ds(0, size), :]
            i = n * 7 + d - 1
            cs.append(put(ref, ref, rowsend.at[i], rowrecv.at[i], ac((code + d) % 8)))
        for c in cs:
            c.wait_recv()
        out = unpack(merge([xrow[n, q, 0:32, :] for q in range(8)]))
        if extra is None:
            return out
        return out, total([xrow[n, q, 32:40, :] for q in range(8)])[0:1, 0:1]

    def one_axis(n, buf, me, ssem, rsem, dev, val, extra, merge):
        buf[n, me, 0:64, :] = val
        size = 64
        if extra is not None:
            buf[n, me, 64:72, :] = jnp.broadcast_to(extra, (8, 128))
            size = 72
        cs = []
        for d in range(1, 4):
            ref = buf.at[n, me, pl.ds(0, size), :]
            i = n * 3 + d - 1
            cs.append(put(ref, ref, ssem.at[i], rsem.at[i], dev(d)))
        for c in cs:
            c.wait_recv()
        out = merge([buf[n, q, 0:64, :] for q in range(4)])
        if extra is None:
            return out, None
        return out, total([buf[n, q, 64:72, :] for q in range(4)])[0:1, 0:1]

    def col_exchange(n, val, extra, merge):
        val, extra = one_axis(n, xy, y, ysend, yrecv, lambda d: at(z, y + d), val, extra, merge)
        return one_axis(n, xz, z, zsend, zrecv, lambda d: at(z + d, y), val, extra, merge)

    turned = jnp.concatenate([wt_ref[...], jnp.ones((96, 128), jnp.float32)], axis=0).T
    wt = jnp.where(lane64 < 32, turned[0:64], pltpu.roll(turned[64:128], 32, 1))
    cap = cap_ref[...]
    wsum = jnp.sum(jnp.where(lane64 < 64, wt, 0.0), keepdims=True)
    csum = jnp.sum(cap, keepdims=True)
    row, capacity = row_exchange(0, row, csum, lse)
    f1 = jnp.log(wt) - row

    def col_first(b, carry):
        f = column(f1, b)
        for k in range(KP):
            c = s_ref[b, :, ks(k)] + f
            m = jnp.max(c, axis=0, keepdims=True)
            tm_ref[rows_at(k, b), :] = m
            ts_ref[rows_at(k, b), :] = jnp.sum(jnp.exp(c - m), axis=0, keepdims=True)
        return carry

    blocks(col_first, 0)

    block = lax.broadcasted_iota(jnp.int32, (128, 128), 0)

    def spread_max(r, acc):
        for u in range(4):
            one = pl.ds(r * 4 + u, 1)
            acc = jnp.maximum(acc, jnp.where(block == tgt_ref[one, :], tm_ref[one, :], NEG))
        return acc

    peak = lax.fori_loop(0, 64, spread_max, jnp.full((128, 128), NEG, jnp.float32))
    peak = jnp.maximum(peak, pltpu.roll(peak, 64, 1))

    lanes = lax.broadcasted_iota(jnp.int32, (256, 128), 1)
    tgt = tgt_ref[...]
    hot = jnp.concatenate(
        [jnp.where(lanes == tgt[:, 0:1], 1.0, 0.0), jnp.where(lanes == tgt[:, 64:65], 1.0, 0.0)], axis=1
    )
    hot_t = jnp.concatenate(
        [hot[:, 0:128].T, hot[:, 128:256].T], axis=1
    ).astype(jnp.bfloat16)
    hot = hot.astype(jnp.bfloat16)

    def hot_dot(one, v):
        out = []
        for _ in range(3):
            h = v.astype(jnp.bfloat16).astype(jnp.float32)
            out.append(h)
            v = v - h
        w = jnp.concatenate(out, axis=1)
        side = (lax.broadcasted_iota(jnp.int32, (1, 384), 1) & 64) == 0
        w = jnp.concatenate([jnp.where(side, w, 0.0), jnp.where(side, 0.0, w)], axis=0)
        o = jnp.dot(one, w.astype(jnp.bfloat16), preferred_element_type=jnp.float32)
        return o[:, 0:128] + (o[:, 128:256] + o[:, 256:384])

    def spread_out(v):
        return hot_dot(hot, v)

    def collect(v):
        o = hot_dot(hot_t, v)
        return o + pltpu.roll(o, 64, 1)

    def compact(v):
        return jnp.where(left, v[0:64], v[64:128])

    def expand(c):
        r = pltpu.roll(c, 64, 1)
        return jnp.concatenate([jnp.where(left, c, r), jnp.where(left, r, c)], axis=0)

    tiles = ts_ref[...] * jnp.exp(tm_ref[...] - spread_out(peak))
    sums = collect(tiles)
    some = sums > 0.0
    col = jnp.where(some, peak + jnp.log(jnp.where(some, sums, 1.0)), NEG)
    col, weight = col_exchange(0, compact(col), wsum, lse)
    lw = jnp.log(weight)
    f1 = f1 - lw
    g1 = jnp.log(cap) - jnp.log(capacity) - (col - lw)
    amass = wt / weight
    bmass = cap / capacity

    tm_ref[...] = spread_out(expand(g1))

    def first_rows(b, acc):
        f = column(f1, b)
        t = None
        for k in range(KP):
            e = jnp.exp(s_ref[b, :, ks(k)] + f + tm_ref[rows_at(k, b), :])
            s_ref[b, :, ks(k)] = e
            t = e if t is None else t + e
        return jnp.where(lane64 == home(b), jnp.sum(t, axis=1, keepdims=True), acc)

    row = blocks(first_rows, jnp.ones((64, 128), jnp.float32))
    u = amass / row_exchange(1, row, None, total)

    def cols(u):
        def body(b, carry):
            c = column(u, b)
            for k in range(KP):
                ts_ref[rows_at(k, b), :] = jnp.sum(s_ref[b, :, ks(k)] * c, axis=0, keepdims=True)
            return carry

        blocks(body, 0)
        return compact(collect(ts_ref[...]))

    v = bmass / col_exchange(1, cols(u), None, total)[0]

    tm_ref[...] = spread_out(expand(v))

    def rows(b, acc):
        t = functools.reduce(
            jnp.add, [s_ref[b, :, ks(k)] * tm_ref[rows_at(k, b), :] for k in range(KP)]
        )
        return jnp.where(lane64 == home(b), jnp.sum(t, axis=1, keepdims=True), acc)

    row = blocks(rows, jnp.ones((64, 128), jnp.float32))
    u = amass / row_exchange(2, row, None, total)
    f = f1 + jnp.log(u)
    fout_ref[...] = jnp.concatenate([f, pltpu.roll(f, 96, 1)], axis=0).T[0:32]
    v = bmass / col_exchange(2, cols(u), None, total)[0]
    gout_ref[...] = g1 + jnp.log(v)

    for c in sends:
        c.wait_send()


def body(residuals, codebook, item_weight, code_capacity, pairs):
    items = residuals.shape[1]
    codes = codebook.shape[1]
    vm = pl.BlockSpec(memory_space=pltpu.VMEM)
    hbm = pl.BlockSpec(memory_space=pl.ANY)
    f32, bf16 = jnp.float32, jnp.bfloat16
    dma = pltpu.SemaphoreType.DMA
    f, g = pl.pallas_call(
        kernel,
        out_shape=[jax.ShapeDtypeStruct((32, 128), f32), jax.ShapeDtypeStruct((64, 128), f32)],
        in_specs=[hbm, hbm, vm, vm, vm],
        out_specs=[vm, vm],
        scratch_shapes=[
            pltpu.VMEM((16, 2, 8, codes), f32),
            pltpu.VMEM((8, 32, items), f32),
            pltpu.VMEM((128, 16, 16, 128), bf16),
            pltpu.VMEM((128, 16, 16, 128), bf16),
            pltpu.VMEM((64, 128, 256), bf16),
            pltpu.VMEM((64, 64, 512), f32),
            pltpu.VMEM((64, 128), jnp.int32),
            pltpu.VMEM((256, 128), jnp.int32),
            pltpu.VMEM((64, 128), jnp.int32),
            pltpu.SMEM((64, 128), jnp.int32),
            pltpu.VMEM((256, 128), f32),
            pltpu.VMEM((256, 128), f32),
            pltpu.VMEM((3, 8, 40, 128), f32),
            pltpu.VMEM((3, 4, 72, 128), f32),
            pltpu.VMEM((3, 4, 72, 128), f32),
            dma((40,)),
            dma((40,)),
            dma((8,)),
            dma((8,)),
            dma((4,)),
            dma((21,)),
            dma((21,)),
            dma((9,)),
            dma((9,)),
            dma((9,)),
            dma((9,)),
        ],
        compiler_params=pltpu.CompilerParams(
            collective_id=0, has_side_effects=True, vmem_limit_bytes=60 * 1024 * 1024
        ),
    )(
        codebook.reshape(2, 8, codes),
        residuals,
        item_weight.reshape(32, 128),
        code_capacity.reshape(64, 128),
        pairs,
    )
    return f.reshape(items), g.reshape(codes)


def solution(mesh):
    placed = (P("code", "item"), P("item", "code"), P("item"), P("code"), P("item", "code"))
    return jax.shard_map(
        body, mesh=mesh, in_specs=placed, out_specs=(P("item"), P("code")), check_vma=False
    )
```

```python
import functools
import math

import jax
import jax.numpy as jnp
from jax import lax
from jax.experimental import pallas as pl
from jax.experimental.pallas import tpu as pltpu
from jax.sharding import PartitionSpec as P

BLOCK = 64
SLOTS = 8
KP = SLOTS // 2
NEG = -1e30
ORDER = [(0, 0), (0, 3), (3, 0), (0, 1), (1, 0), (0, 2), (2, 0), (3, 3), (1, 3), (3, 1), (1, 1), (3, 2), (2, 3), (1, 2), (2, 1), (2, 2)]
SOFTNESS = 0.1
MESH = pl.DeviceIdType.MESH


def kernel(
    cb_ref,
    res_ref,
    wt_ref,
    cap_ref,
    pairs_ref,
    fout_ref,
    gout_ref,
    cg,
    rg,
    vh,
    vl,
    rt,
    s_ref,
    padded,
    tgt_ref,
    ids_v,
    ids_ref,
    tm_ref,
    ts_ref,
    xrow,
    xy,
    xz,
    csend,
    crecv,
    rsend,
    rrecv,
    lsem,
    rowsend,
    rowrecv,
    ysend,
    yrecv,
    zsend,
    zrecv,
):
    item = lax.axis_index("item")
    code = lax.axis_index("code")
    z, y = item // 4, item % 4
    x, core = code // 2, code % 2
    cd = cg.shape[3]
    idv = rg.shape[2]
    width = 256
    scale = 1.0 / (SOFTNESS * math.sqrt(width))

    def at(zz, yy):
        return {"item": (zz % 4) * 4 + yy % 4, "code": code}

    def ac(cc):
        return {"item": item, "code": cc}

    bar = pltpu.get_barrier_semaphore()
    for d in range(1, 4):
        pl.semaphore_signal(bar, inc=1, device_id=at(z, y + d), device_id_type=MESH)
        pl.semaphore_signal(bar, inc=1, device_id=at(z + d, y), device_id_type=MESH)
    for d in range(1, 8):
        pl.semaphore_signal(bar, inc=1, device_id=ac((code + d) % 8), device_id_type=MESH)

    lane = lax.broadcasted_iota(jnp.int32, (1, 128), 1)
    left = lane < 64
    lane64 = lax.broadcasted_iota(jnp.int32, (64, 128), 1)
    padded[...] = jnp.full((64, 128), -1, jnp.int32)
    padded[:, 0:16] = pairs_ref[...]
    named = padded[...]
    live = jnp.where(named >= 0, 1, 0)
    count = live
    for sh in (1, 2, 4, 8):
        count = count + jnp.where(lane64 >= sh, pltpu.roll(count, sh, 1), 0)
    count = live * count
    picked = []
    ids = jnp.zeros((64, 128), jnp.int32)
    for k in range(SLOTS):
        one = jnp.max(jnp.where(count == k + 1, named, -1), axis=1, keepdims=True)
        ids = jnp.where(lane64 == k, jnp.maximum(one, 0) ^ (k & 1), ids)
        picked.append(jnp.where(one < 0, -1, (one >> 1) + (one & 1) * 64))
    for k in range(KP):
        tgt_ref[k * 64 : k * 64 + 64, :] = jnp.where(left, picked[2 * k], picked[2 * k + 1])
    ids_v[...] = ids
    idc = pltpu.make_async_copy(ids_v, ids_ref, lsem.at[3])
    idc.start()
    idc.wait()
    pl.semaphore_wait(bar, 13)

    half = cd // 2
    sends = []

    def put(src, dst, ss, rs, dev):
        c = pltpu.make_async_remote_copy(
            src_ref=src, dst_ref=dst, send_sem=ss, recv_sem=rs, device_id=dev, device_id_type=MESH
        )
        c.start()
        sends.append(c)
        return c

    def place(h, p, s):
        zz, yy = (s, p) if h == 0 else (p, s)
        return (zz % 4) * 4 + yy % 4

    def where_to(h, p, s):
        zz, yy = (s, p) if h == 0 else (p, s)
        return at(zz, yy)

    pos = [(y, z), (z, y)]
    cnt = [0]

    def cput(h, src_ps, c, to, own=False):
        i = cnt[0]
        cnt[0] += 1
        col = pl.ds(c * half, half)
        dst = cg.at[place(h, *src_ps), h, :, col]
        src = cb_ref.at[h, :, col] if own else dst
        return put(src, dst, csend.at[i], crecv.at[i], where_to(h, *to))

    def first(d):
        return 0 if d > 0 else 1

    dirs = [(h, d) for d in (1, -1) for h in range(2)]
    prim, sec = {}, {}
    locals_ = []
    for turn in range(2):
        for h, d in dirs:
            p, s = pos[h]
            c = first(d) ^ turn
            prim[h, d, c] = cput(h, (p, s), c, (p + d, s), True)
        for h, d in dirs:
            p, s = pos[h]
            c = first(d) ^ turn
            sec[h, 0, d, c] = cput(h, (p, s), c, (p, s + d), True)
    for h in range(2):
        lc = pltpu.make_async_copy(cb_ref.at[h], cg.at[item, h], lsem.at[h])
        lc.start()
        locals_.append(lc)

    rhalf = idv // 2
    rcnt = [0]

    def rdev(xx):
        return (xx % 4) * 2 + core

    def rput(xx, cols, to, own=False):
        i = rcnt[0]
        rcnt[0] += 1
        d = rdev(xx)
        if cols is None:
            dst = rg.at[pl.ds(2 * d, 2)]
        else:
            dst = rg.at[pl.ds(2 * d, 2), :, pl.ds(cols * rhalf, rhalf)]
        return put(res_ref if own else dst, dst, rsend.at[i], rrecv.at[i], ac(to))

    other = x * 2 + (1 - core)
    rp = {}
    rp[1] = rput(x, None, rdev(x + 1), True)
    rp[-1] = rput(x, None, rdev(x - 1), True)
    rc = [rput(x, None, other, True)]
    lc = pltpu.make_async_copy(res_ref, rg.at[pl.ds(2 * code, 2)], lsem.at[2])
    lc.start()
    locals_.append(lc)

    UN = 8
    leftw = lax.broadcasted_iota(jnp.int32, (width // 2, 128), 1) < 64

    def rows_at(k, b):
        return pl.ds(k * 64 + b, 1)

    def home(b):
        return (b & 1) * 32 + (b >> 1)

    def column(f, b):
        return jnp.sum(jnp.where(lane64 == home(b), f, 0.0), axis=1, keepdims=True)

    def ks(k):
        return slice(k * 128, k * 128 + 128)

    def blocks(body, init, un=UN):
        def step(j, acc):
            for r in range(un):
                acc = body(j * un + r, acc)
            return acc

        return lax.fori_loop(0, 64 // un, step, init)

    def score_part(b, part):
        r8 = pl.ds(part * 8, 8)
        wh, wl = [], []
        for k in range(KP):
            i0 = ids_ref[b, 2 * k]
            i1 = ids_ref[b, 2 * k + 1]
            for ref, out in ((vh, wh), (vl, wl)):
                one = ref[i0, r8].reshape(width // 2, 128)
                two = ref[i1, r8].reshape(width // 2, 128)
                out.append(jnp.where(leftw, one, two))
        a = rt[b, :, part * 128 : part * 128 + 128]
        ss = []
        for k in range(0, KP, 2):
            d1 = jnp.dot(a, jnp.concatenate(wh[k : k + 2], axis=1), preferred_element_type=jnp.float32)
            d2 = jnp.dot(
                a[0:64], jnp.concatenate(wl[k : k + 2], axis=1), preferred_element_type=jnp.float32
            )
            t = d1[0:64] + (d1[64:128] + d2)
            ss += [t[:, 0:128], t[:, 128:256]]
        return ss

    def score_half(g):
        for r in range(8):
            b = g * 8 + r
            for k, t in enumerate(score_part(b, 0)):
                s_ref[b, :, ks(k)] = t

    tasks = []
    parts = {}
    ready = [0]

    def split_items(c, carry):
        col = pl.ds(pl.multiple_of(c * 128, 128), 128)
        v = jnp.concatenate([rg[source(k), :, col] for k in ORDER], axis=0).T * scale
        hi = v.astype(jnp.bfloat16)
        lo = (v - hi.astype(jnp.float32)).astype(jnp.bfloat16)
        for b in range(2):
            rt[2 * c + b, 0:64, :] = hi[b * 64 : b * 64 + 64]
            rt[2 * c + b, 64:128, :] = lo[b * 64 : b * 64 + 64]
        return carry

    def source(key):
        return ((z + key[1]) % 4) * 4 + (y + key[0]) % 4

    def split_codes(d, rank):
        def step(j, carry):
            for r in range(8):
                q = j * 8 + r
                col = pl.ds(pl.multiple_of(q * 128, 128), 128)
                v = cg[d, :, :, col].reshape(16, 128)
                for b, t in ((0, v), (1, pltpu.roll(v, 64, 1))):
                    hi = t.astype(jnp.bfloat16)
                    vh[2 * q + b, rank] = hi
                    vl[2 * q + b, rank] = (t - hi.astype(jnp.float32)).astype(jnp.bfloat16)
            return carry

        lax.fori_loop(0, cd // 1024, step, 0)

    def got(h, op, os, share):
        dy, dz = ((op, os) if h == 0 else (os, op))
        key = dy % 4, dz % 4
        parts[key] = parts.get(key, 0) + share
        if parts[key] == 4:
            r = ready[0]
            ready[0] += 1
            assert ORDER[r] == key
            tasks.append(lambda: split_codes(source(key), r))
            if r == 7:
                for g in range(8):
                    tasks.append(lambda g=g: score_half(g))

    def work(n):
        for _ in range(min(n, len(tasks))):
            tasks.pop(0)()

    ph, sh = {}, {}
    offs = {0: 0, 1: -1, -1: 1, 2: 2}

    def pass_on(h, k, c):
        p, s = pos[h]
        for d in (1, -1) if c == 0 else (-1, 1):
            sec[h, k, d, c] = cput(h, (p + offs[k], s), c, (p, s + d))

    def forward(k):
        for h, d in dirs:
            p, s = pos[h]
            c = first(d)
            if k:
                work(1)
            sec[h, k, d, c].wait_recv()
            sh[h, k, d] = cput(h, (p + offs[k], s - d), c, (p, s + d))
            got(h, offs[k], -d, 1)

    def take(k, turn):
        for h, d in dirs:
            work(1)
            if turn:
                sec[h, k, d, 1 - first(d)].wait_recv()
                got(h, offs[k], -d, 1)
            else:
                sh[h, k, d].wait_recv()
                got(h, offs[k], 2, 1)

    for h, d in dirs:
        p, s = pos[h]
        c = first(d)
        prim[h, d, c].wait_recv()
        ph[h, d] = cput(h, (p - d, s), c, (p + d, s))
        pass_on(h, d, c)
        got(h, -d, 0, 1)
    forward(0)
    for h, d in dirs:
        c = 1 - first(d)
        prim[h, d, c].wait_recv()
        pass_on(h, d, c)
        got(h, -d, 0, 1)
    for d in (1, -1):
        rp[d].wait_recv()
        rp[2 * d] = rput(x - d, 0 if d > 0 else 1, rdev(x + d))
        rc.append(rput(x - d, None, other))
    for h, d in dirs:
        ph[h, d].wait_recv()
        pass_on(h, 2, first(d))
        got(h, 2, 0, 1)
    for c in locals_:
        c.wait()
    for h in range(2):
        got(h, 0, 0, 2)
    take(0, 1)
    rp[2].wait_recv()
    rp[-2].wait_recv()
    rc.append(rput(x + 2, None, other))
    forward(1)
    forward(-1)
    for c in rc:
        c.wait_recv()
    for g in range(8):
        n = idv // 128 // 8
        tasks.append(lambda g=g, n=n: lax.fori_loop(g * n, g * n + n, split_items, 0))
    take(0, 0)
    take(1, 1)
    take(-1, 1)
    forward(2)
    take(2, 1)
    for k in (1, -1, 2):
        take(k, 0)
    work(len(tasks))

    def score_block(b, acc):
        ss = score_part(b, 1)
        for k in range(KP):
            ss[k] = jnp.where(tgt_ref[rows_at(k, b), :] >= 0, ss[k] + s_ref[b, :, ks(k)], NEG)
            s_ref[b, :, ks(k)] = ss[k]
        m = jnp.max(functools.reduce(jnp.maximum, ss), axis=1, keepdims=True)
        t = functools.reduce(jnp.add, [jnp.exp(s - m) for s in ss])
        t = jnp.sum(t, axis=1, keepdims=True)
        return jnp.where(lane64 == home(b), m + jnp.log(t), acc)

    row = blocks(score_block, jnp.zeros((64, 128), jnp.float32), 8)

    lane32 = lax.broadcasted_iota(jnp.int32, (32, 128), 1) < 64

    def pack(r):
        return jnp.where(lane32, r[0:32], pltpu.roll(r[32:64], 64, 1))

    def unpack(m):
        return jnp.concatenate([m, pltpu.roll(m, 64, 1)], axis=0)

    def lse(parts):
        m = functools.reduce(jnp.maximum, parts)
        t = functools.reduce(jnp.add, [jnp.exp(q - m) for q in parts])
        return m + jnp.log(t)

    def total(parts):
        return functools.reduce(jnp.add, parts)

    def row_exchange(n, r, extra, merge):
        xrow[n, code, 0:32, :] = pack(r)
        size = 32
        if extra is not None:
            xrow[n, code, 32:40, :] = jnp.broadcast_to(extra, (8, 128))
            size = 40
        cs = []
        for d in range(1, 8):
            ref = xrow.at[n, code, pl.ds(0, size), :]
            i = n * 7 + d - 1
            cs.append(put(ref, ref, rowsend.at[i], rowrecv.at[i], ac((code + d) % 8)))
        for c in cs:
            c.wait_recv()
        out = unpack(merge([xrow[n, q, 0:32, :] for q in range(8)]))
        if extra is None:
            return out
        return out, total([xrow[n, q, 32:40, :] for q in range(8)])[0:1, 0:1]

    def one_axis(n, buf, me, ssem, rsem, dev, val, extra, merge):
        buf[n, me, 0:64, :] = val
        size = 64
        if extra is not None:
            buf[n, me, 64:72, :] = jnp.broadcast_to(extra, (8, 128))
            size = 72
        cs = []
        for d in range(1, 4):
            ref = buf.at[n, me, pl.ds(0, size), :]
            i = n * 3 + d - 1
            cs.append(put(ref, ref, ssem.at[i], rsem.at[i], dev(d)))
        for c in cs:
            c.wait_recv()
        out = merge([buf[n, q, 0:64, :] for q in range(4)])
        if extra is None:
            return out, None
        return out, total([buf[n, q, 64:72, :] for q in range(4)])[0:1, 0:1]

    def col_exchange(n, val, extra, merge):
        val, extra = one_axis(n, xy, y, ysend, yrecv, lambda d: at(z, y + d), val, extra, merge)
        return one_axis(n, xz, z, zsend, zrecv, lambda d: at(z + d, y), val, extra, merge)

    turned = jnp.concatenate([wt_ref[...], jnp.ones((96, 128), jnp.float32)], axis=0).T
    wt = jnp.where(lane64 < 32, turned[0:64], pltpu.roll(turned[64:128], 32, 1))
    cap = cap_ref[...]
    wsum = jnp.sum(jnp.where(lane64 < 64, wt, 0.0), keepdims=True)
    csum = jnp.sum(cap, keepdims=True)
    row, capacity = row_exchange(0, row, csum, lse)
    f1 = jnp.log(wt) - row

    def col_first(b, carry):
        f = column(f1, b)
        for k in range(KP):
            c = s_ref[b, :, ks(k)] + f
            m = jnp.max(c, axis=0, keepdims=True)
            tm_ref[rows_at(k, b), :] = m
            ts_ref[rows_at(k, b), :] = jnp.sum(jnp.exp(c - m), axis=0, keepdims=True)
        return carry

    blocks(col_first, 0)

    block = lax.broadcasted_iota(jnp.int32, (128, 128), 0)

    def spread_max(r, acc):
        for u in range(4):
            one = pl.ds(r * 4 + u, 1)
            acc = jnp.maximum(acc, jnp.where(block == tgt_ref[one, :], tm_ref[one, :], NEG))
        return acc

    peak = lax.fori_loop(0, 64, spread_max, jnp.full((128, 128), NEG, jnp.float32))
    peak = jnp.maximum(peak, pltpu.roll(peak, 64, 1))

    lanes = lax.broadcasted_iota(jnp.int32, (256, 128), 1)
    tgt = tgt_ref[...]
    hot = jnp.concatenate(
        [jnp.where(lanes == tgt[:, 0:1], 1.0, 0.0), jnp.where(lanes == tgt[:, 64:65], 1.0, 0.0)], axis=1
    )
    hot_t = jnp.concatenate(
        [hot[:, 0:128].T, hot[:, 128:256].T], axis=1
    ).astype(jnp.bfloat16)
    hot = hot.astype(jnp.bfloat16)

    def hot_dot(one, v):
        out = []
        for _ in range(3):
            h = v.astype(jnp.bfloat16).astype(jnp.float32)
            out.append(h)
            v = v - h
        w = jnp.concatenate(out, axis=1)
        side = (lax.broadcasted_iota(jnp.int32, (1, 384), 1) & 64) == 0
        w = jnp.concatenate([jnp.where(side, w, 0.0), jnp.where(side, 0.0, w)], axis=0)
        o = jnp.dot(one, w.astype(jnp.bfloat16), preferred_element_type=jnp.float32)
        return o[:, 0:128] + (o[:, 128:256] + o[:, 256:384])

    def spread_out(v):
        return hot_dot(hot, v)

    def collect(v):
        o = hot_dot(hot_t, v)
        return o + pltpu.roll(o, 64, 1)

    def compact(v):
        return jnp.where(left, v[0:64], v[64:128])

    def expand(c):
        r = pltpu.roll(c, 64, 1)
        return jnp.concatenate([jnp.where(left, c, r), jnp.where(left, r, c)], axis=0)

    tiles = ts_ref[...] * jnp.exp(tm_ref[...] - spread_out(peak))
    sums = collect(tiles)
    some = sums > 0.0
    col = jnp.where(some, peak + jnp.log(jnp.where(some, sums, 1.0)), NEG)
    col, weight = col_exchange(0, compact(col), wsum, lse)
    lw = jnp.log(weight)
    f1 = f1 - lw
    g1 = jnp.log(cap) - jnp.log(capacity) - (col - lw)
    amass = wt / weight
    bmass = cap / capacity

    tm_ref[...] = spread_out(expand(g1))

    def first_rows(b, acc):
        f = column(f1, b)
        t = None
        for k in range(KP):
            e = jnp.exp(s_ref[b, :, ks(k)] + f + tm_ref[rows_at(k, b), :])
            s_ref[b, :, ks(k)] = e
            t = e if t is None else t + e
        return jnp.where(lane64 == home(b), jnp.sum(t, axis=1, keepdims=True), acc)

    row = blocks(first_rows, jnp.ones((64, 128), jnp.float32))
    u = amass / row_exchange(1, row, None, total)

    def cols(u):
        def body(b, carry):
            c = column(u, b)
            for k in range(KP):
                ts_ref[rows_at(k, b), :] = jnp.sum(s_ref[b, :, ks(k)] * c, axis=0, keepdims=True)
            return carry

        blocks(body, 0)
        return compact(collect(ts_ref[...]))

    v = bmass / col_exchange(1, cols(u), None, total)[0]

    tm_ref[...] = spread_out(expand(v))

    def rows(b, acc):
        t = functools.reduce(
            jnp.add, [s_ref[b, :, ks(k)] * tm_ref[rows_at(k, b), :] for k in range(KP)]
        )
        return jnp.where(lane64 == home(b), jnp.sum(t, axis=1, keepdims=True), acc)

    row = blocks(rows, jnp.ones((64, 128), jnp.float32))
    u = amass / row_exchange(2, row, None, total)
    f = f1 + jnp.log(u)
    fout_ref[...] = jnp.concatenate([f, pltpu.roll(f, 96, 1)], axis=0).T[0:32]
    v = bmass / col_exchange(2, cols(u), None, total)[0]
    gout_ref[...] = g1 + jnp.log(v)

    for c in sends:
        c.wait_send()


def body(residuals, codebook, item_weight, code_capacity, pairs):
    items = residuals.shape[1]
    codes = codebook.shape[1]
    vm = pl.BlockSpec(memory_space=pltpu.VMEM)
    hbm = pl.BlockSpec(memory_space=pl.ANY)
    f32, bf16 = jnp.float32, jnp.bfloat16
    dma = pltpu.SemaphoreType.DMA
    f, g = pl.pallas_call(
        kernel,
        out_shape=[jax.ShapeDtypeStruct((32, 128), f32), jax.ShapeDtypeStruct((64, 128), f32)],
        in_specs=[hbm, hbm, vm, vm, vm],
        out_specs=[vm, vm],
        scratch_shapes=[
            pltpu.VMEM((16, 2, 8, codes), f32),
            pltpu.VMEM((16, 16, items), f32),
            pltpu.VMEM((128, 16, 16, 128), bf16),
            pltpu.VMEM((128, 16, 16, 128), bf16),
            pltpu.VMEM((64, 128, 256), bf16),
            pltpu.VMEM((64, 64, 512), f32),
            pltpu.VMEM((64, 128), jnp.int32),
            pltpu.VMEM((256, 128), jnp.int32),
            pltpu.VMEM((64, 128), jnp.int32),
            pltpu.SMEM((64, 128), jnp.int32),
            pltpu.VMEM((256, 128), f32),
            pltpu.VMEM((256, 128), f32),
            pltpu.VMEM((3, 8, 40, 128), f32),
            pltpu.VMEM((3, 4, 72, 128), f32),
            pltpu.VMEM((3, 4, 72, 128), f32),
            dma((64,)),
            dma((64,)),
            dma((8,)),
            dma((8,)),
            dma((4,)),
            dma((21,)),
            dma((21,)),
            dma((9,)),
            dma((9,)),
            dma((9,)),
            dma((9,)),
        ],
        compiler_params=pltpu.CompilerParams(
            collective_id=0, has_side_effects=True, vmem_limit_bytes=60 * 1024 * 1024
        ),
    )(
        codebook.reshape(2, 8, codes),
        residuals.reshape(2, 16, items),
        item_weight.reshape(32, 128),
        code_capacity.reshape(64, 128),
        pairs,
    )
    return f.reshape(items), g.reshape(codes)


def solution(mesh):
    placed = (P("code", "item"), P("item", "code"), P("item"), P("code"), P("item", "code"))
    return jax.shard_map(
        body, mesh=mesh, in_specs=placed, out_specs=(P("item"), P("code")), check_vma=False
    )
```

```python
import functools
import math

import jax
import jax.numpy as jnp
from jax import lax
from jax.experimental import pallas as pl
from jax.experimental.pallas import tpu as pltpu
from jax.sharding import PartitionSpec as P

BLOCK = 64
SLOTS = 8
KP = SLOTS // 2
NEG = -1e30
PARTS = 2
LANES = 64 // PARTS
ORDER = [(0, 0), (0, 3), (3, 0), (0, 1), (1, 0), (0, 2), (2, 0), (3, 3), (1, 3), (3, 1), (1, 1), (3, 2), (2, 3), (1, 2), (2, 1), (2, 2)]
SOFTNESS = 0.1
MESH = pl.DeviceIdType.MESH


def kernel(
    cb_ref,
    res_ref,
    wt_ref,
    cap_ref,
    pairs_ref,
    fout_ref,
    gout_ref,
    cg,
    rg,
    vh,
    vl,
    rt,
    s_ref,
    slots,
    padded,
    tgt_ref,
    ids_v,
    ids_ref,
    tm_ref,
    ts_ref,
    xrow,
    xy,
    xz,
    csend,
    crecv,
    rsend,
    rrecv,
    lsem,
    rowsend,
    rowrecv,
    ysend,
    yrecv,
    zsend,
    zrecv,
):
    item = lax.axis_index("item")
    code = lax.axis_index("code")
    z, y = item // 4, item % 4
    x, core = code // 2, code % 2
    cd = cg.shape[3]
    idv = rg.shape[2]
    width = 256
    scale = 1.0 / (SOFTNESS * math.sqrt(width))

    def at(zz, yy):
        return {"item": (zz % 4) * 4 + yy % 4, "code": code}

    def ac(cc):
        return {"item": item, "code": cc}

    bar = pltpu.get_barrier_semaphore()
    for d in range(1, 4):
        pl.semaphore_signal(bar, inc=1, device_id=at(z, y + d), device_id_type=MESH)
        pl.semaphore_signal(bar, inc=1, device_id=at(z + d, y), device_id_type=MESH)
    for d in range(1, 8):
        pl.semaphore_signal(bar, inc=1, device_id=ac((code + d) % 8), device_id_type=MESH)

    lane = lax.broadcasted_iota(jnp.int32, (1, 128), 1)
    left = lane < 64
    lane64 = lax.broadcasted_iota(jnp.int32, (64, 128), 1)
    sc = pltpu.make_async_copy(pairs_ref, slots, lsem.at[3])
    sc.start()
    padded[...] = jnp.full((128, 128), -1, jnp.int32)
    sc.wait()
    padded[0:16, 0:64] = slots[...]
    named = padded[...].T[0:64]
    live = jnp.where(named >= 0, 1, 0)
    count = live
    for sh in (1, 2, 4, 8):
        count = count + jnp.where(lane64 >= sh, pltpu.roll(count, sh, 1), 0)
    count = live * count
    picked = []
    ids = jnp.zeros((64, 128), jnp.int32)
    for k in range(SLOTS):
        one = jnp.max(jnp.where(count == k + 1, named, -1), axis=1, keepdims=True)
        ids = jnp.where(lane64 == k, jnp.maximum(one, 0) ^ (k & 1), ids)
        picked.append(jnp.where(one < 0, -1, (one >> 1) + (one & 1) * 64))
    for k in range(KP):
        tgt_ref[k * 64 : k * 64 + 64, :] = jnp.where(left, picked[2 * k], picked[2 * k + 1])
    ids_v[...] = ids
    idc = pltpu.make_async_copy(ids_v, ids_ref, lsem.at[3])
    idc.start()
    idc.wait()
    pl.semaphore_wait(bar, 13)

    half = cd // 2
    sends = []

    def put(src, dst, ss, rs, dev):
        c = pltpu.make_async_remote_copy(
            src_ref=src, dst_ref=dst, send_sem=ss, recv_sem=rs, device_id=dev, device_id_type=MESH
        )
        c.start()
        sends.append(c)
        return c

    def place(h, p, s):
        zz, yy = (s, p) if h == 0 else (p, s)
        return (zz % 4) * 4 + yy % 4

    def where_to(h, p, s):
        zz, yy = (s, p) if h == 0 else (p, s)
        return at(zz, yy)

    pos = [(y, z), (z, y)]
    cnt = [0]

    def cput(h, src_ps, c, to, own=False):
        i = cnt[0]
        cnt[0] += 1
        col = pl.ds(c * half, half)
        dst = cg.at[place(h, *src_ps), h, :, col]
        src = cb_ref.at[h, :, col] if own else dst
        return put(src, dst, csend.at[i], crecv.at[i], where_to(h, *to))

    def first(d):
        return 0 if d > 0 else 1

    dirs = [(h, d) for d in (1, -1) for h in range(2)]
    prim, sec = {}, {}
    locals_ = []
    for turn in range(2):
        for h, d in dirs:
            p, s = pos[h]
            c = first(d) ^ turn
            prim[h, d, c] = cput(h, (p, s), c, (p + d, s), True)
        for h, d in dirs:
            p, s = pos[h]
            c = first(d) ^ turn
            sec[h, 0, d, c] = cput(h, (p, s), c, (p, s + d), True)
    for h in range(2):
        lc = pltpu.make_async_copy(cb_ref.at[h], cg.at[item, h], lsem.at[h])
        lc.start()
        locals_.append(lc)

    rhalf = idv // 2
    rcnt = [0]

    def rdev(xx):
        return (xx % 4) * 2 + core

    def rput(xx, cols, to, own=False):
        i = rcnt[0]
        rcnt[0] += 1
        d = rdev(xx)
        if cols is None:
            dst = rg.at[pl.ds(2 * d, 2)]
        else:
            dst = rg.at[pl.ds(2 * d, 2), :, pl.ds(cols * rhalf, rhalf)]
        return put(res_ref if own else dst, dst, rsend.at[i], rrecv.at[i], ac(to))

    other = x * 2 + (1 - core)
    rp = {}
    rp[1] = rput(x, None, rdev(x + 1), True)
    rp[-1] = rput(x, None, rdev(x - 1), True)
    rc = [rput(x, None, other, True)]
    lc = pltpu.make_async_copy(res_ref, rg.at[pl.ds(2 * code, 2)], lsem.at[2])
    lc.start()
    locals_.append(lc)

    UN = 8
    leftw = lax.broadcasted_iota(jnp.int32, (width // 2, 128), 1) < 64

    def rows_at(k, b):
        return pl.ds(k * 64 + b, 1)

    def column(f, at):
        return jnp.sum(jnp.where(lane64 == at, f, 0.0), axis=1, keepdims=True)

    def ks(k):
        return slice(k * 128, k * 128 + 128)

    def blocks(part, body, init, un=UN):
        low = part * LANES

        def step(j, acc):
            for r in range(un):
                i = j * un + r
                acc = body(2 * (low % 32 + i) + low // 32, low + i, acc)
            return acc

        return lax.fori_loop(0, LANES // un, step, init)

    def score_part(b, part):
        r8 = pl.ds(part * 8, 8)
        wh, wl = [], []
        for k in range(KP):
            i0 = ids_ref[b, 2 * k]
            i1 = ids_ref[b, 2 * k + 1]
            for ref, out in ((vh, wh), (vl, wl)):
                one = ref[i0, r8].reshape(width // 2, 128)
                two = ref[i1, r8].reshape(width // 2, 128)
                out.append(jnp.where(leftw, one, two))
        a = rt[b, :, part * 128 : part * 128 + 128]
        ss = []
        for k in range(0, KP, 2):
            d1 = jnp.dot(a, jnp.concatenate(wh[k : k + 2], axis=1), preferred_element_type=jnp.float32)
            d2 = jnp.dot(
                a[0:64], jnp.concatenate(wl[k : k + 2], axis=1), preferred_element_type=jnp.float32
            )
            t = d1[0:64] + (d1[64:128] + d2)
            ss += [t[:, 0:128], t[:, 128:256]]
        return ss

    def score_half(g):
        for r in range(8):
            b = g * 8 + r
            for k, t in enumerate(score_part(b, 0)):
                s_ref[b, :, ks(k)] = t

    tasks = []
    parts = {}
    ready = [0]

    def split_items(c, carry):
        col = pl.ds(pl.multiple_of(c * 128, 128), 128)
        v = jnp.concatenate([rg[source(k), :, col] for k in ORDER], axis=0).T * scale
        hi = v.astype(jnp.bfloat16)
        lo = (v - hi.astype(jnp.float32)).astype(jnp.bfloat16)
        for b in range(2):
            rt[2 * c + b, 0:64, :] = hi[b * 64 : b * 64 + 64]
            rt[2 * c + b, 64:128, :] = lo[b * 64 : b * 64 + 64]
        return carry

    def source(key):
        return ((z + key[1]) % 4) * 4 + (y + key[0]) % 4

    def split_codes(d, rank):
        def step(j, carry):
            for r in range(8):
                q = j * 8 + r
                col = pl.ds(pl.multiple_of(q * 128, 128), 128)
                v = cg[d, :, :, col].reshape(16, 128)
                for b, t in ((0, v), (1, pltpu.roll(v, 64, 1))):
                    hi = t.astype(jnp.bfloat16)
                    vh[2 * q + b, rank] = hi
                    vl[2 * q + b, rank] = (t - hi.astype(jnp.float32)).astype(jnp.bfloat16)
            return carry

        lax.fori_loop(0, cd // 1024, step, 0)

    def got(h, op, os, share):
        dy, dz = ((op, os) if h == 0 else (os, op))
        key = dy % 4, dz % 4
        parts[key] = parts.get(key, 0) + share
        if parts[key] == 4:
            r = ready[0]
            ready[0] += 1
            assert ORDER[r] == key
            tasks.append(lambda: split_codes(source(key), r))
            if r == 7:
                for g in range(8):
                    tasks.append(lambda g=g: score_half(g))

    def work(n):
        for _ in range(min(n, len(tasks))):
            tasks.pop(0)()

    ph, sh = {}, {}
    offs = {0: 0, 1: -1, -1: 1, 2: 2}

    def pass_on(h, k, c):
        p, s = pos[h]
        for d in (1, -1) if c == 0 else (-1, 1):
            sec[h, k, d, c] = cput(h, (p + offs[k], s), c, (p, s + d))

    def forward(k):
        for h, d in dirs:
            p, s = pos[h]
            c = first(d)
            if k:
                work(1)
            sec[h, k, d, c].wait_recv()
            sh[h, k, d] = cput(h, (p + offs[k], s - d), c, (p, s + d))
            got(h, offs[k], -d, 1)

    def take(k, turn):
        for h, d in dirs:
            work(1)
            if turn:
                sec[h, k, d, 1 - first(d)].wait_recv()
                got(h, offs[k], -d, 1)
            else:
                sh[h, k, d].wait_recv()
                got(h, offs[k], 2, 1)

    for h, d in dirs:
        p, s = pos[h]
        c = first(d)
        prim[h, d, c].wait_recv()
        ph[h, d] = cput(h, (p - d, s), c, (p + d, s))
        pass_on(h, d, c)
        got(h, -d, 0, 1)
    forward(0)
    for h, d in dirs:
        c = 1 - first(d)
        prim[h, d, c].wait_recv()
        pass_on(h, d, c)
        got(h, -d, 0, 1)
    for d in (1, -1):
        rp[d].wait_recv()
        rp[2 * d] = rput(x - d, 0 if d > 0 else 1, rdev(x + d))
        rc.append(rput(x - d, None, other))
    for h, d in dirs:
        ph[h, d].wait_recv()
        pass_on(h, 2, first(d))
        got(h, 2, 0, 1)
    for c in locals_:
        c.wait()
    for h in range(2):
        got(h, 0, 0, 2)
    take(0, 1)
    rp[2].wait_recv()
    rp[-2].wait_recv()
    rc.append(rput(x + 2, None, other))
    forward(1)
    forward(-1)
    for c in rc:
        c.wait_recv()
    for g in range(8):
        n = idv // 128 // 8
        tasks.append(lambda g=g, n=n: lax.fori_loop(g * n, g * n + n, split_items, 0))
    take(0, 0)
    take(1, 1)
    take(-1, 1)
    forward(2)
    take(2, 1)
    for k in (1, -1, 2):
        take(k, 0)
    work(len(tasks))

    def score_block(b, at, acc):
        ss = score_part(b, 1)
        for k in range(KP):
            ss[k] = jnp.where(tgt_ref[rows_at(k, b), :] >= 0, ss[k] + s_ref[b, :, ks(k)], NEG)
            s_ref[b, :, ks(k)] = ss[k]
        m = jnp.max(functools.reduce(jnp.maximum, ss), axis=1, keepdims=True)
        t = functools.reduce(jnp.add, [jnp.exp(s - m) for s in ss])
        t = jnp.sum(t, axis=1, keepdims=True)
        return jnp.where(lane64 == at, m + jnp.log(t), acc)

    def group(g):
        return slice(g * LANES // 2, g * LANES // 2 + LANES // 2)

    def pack(part, r):
        out = r[group(0)] if part == 0 else pltpu.roll(r[group(0)], (-part * LANES) % 128, 1)
        for g in range(1, 128 // LANES):
            shift = ((g - part) * LANES) % 128
            one = pltpu.roll(r[group(g)], shift, 1) if shift else r[group(g)]
            out = jnp.where(lane < g * LANES, out, one)
        return out

    def unpack(part, m):
        out = []
        for g in range(128 // LANES):
            shift = ((part - g) * LANES) % 128
            out.append(pltpu.roll(m, shift, 1) if shift else m)
        return jnp.concatenate(out, axis=0)

    def of_part(part):
        return (lane64 >= part * LANES) & (lane64 < part * LANES + LANES)

    def lse(parts):
        m = functools.reduce(jnp.maximum, parts)
        t = functools.reduce(jnp.add, [jnp.exp(q - m) for q in parts])
        return m + jnp.log(t)

    def total(parts):
        return functools.reduce(jnp.add, parts)

    def row_send(n, part, r, extra=None):
        size = LANES // 2
        xrow[n, part, code, 0:size, :] = pack(part, r)
        if extra is not None:
            xrow[n, part, code, size : size + 8, :] = jnp.broadcast_to(extra, (8, 128))
            size += 8
        cs = []
        for d in range(1, 8):
            ref = xrow.at[n, part, code, pl.ds(0, size), :]
            i = (n * PARTS + part) * 7 + d - 1
            cs.append(put(ref, ref, rowsend.at[i], rowrecv.at[i], ac((code + d) % 8)))
        return cs

    def row_receive(n, part, cs, merge):
        for c in cs:
            c.wait_recv()
        return unpack(part, merge([xrow[n, part, q, 0 : LANES // 2, :] for q in range(8)]))

    def rows_then_cols(n, row_body, extra, merge, finish, col_body):
        sent = []
        for part in range(PARTS):
            r = blocks(part, row_body, jnp.ones((64, 128), jnp.float32))
            sent.append(row_send(n, part, r, extra if part == 0 else None))
        out = jnp.zeros((64, 128), jnp.float32)
        for part in range(PARTS):
            r = row_receive(n, part, sent[part], merge)
            out = jnp.where(of_part(part), finish(r), out)
            blocks(part, functools.partial(col_body, out), 0)
        return out

    def col_exchange(n, val, extra, merge):
        vals = [val[0:32], val[32:64]]
        for stage in range(2):
            cs = []
            for axis, buf, me, ssem, rsem in ((0, xy, y, ysend, yrecv), (1, xz, z, zsend, zrecv)):
                part = axis ^ stage
                size = 32
                buf[n, stage, me, 0:32, :] = vals[part]
                if extra is not None and part == 0:
                    buf[n, stage, me, 32:40, :] = jnp.broadcast_to(extra, (8, 128))
                    size = 40
                for d in (2, 1, 3):
                    ref = buf.at[n, stage, me, pl.ds(0, size), :]
                    i = (n * 2 + stage) * 3 + d - 1
                    dev = at(z, y + d) if axis == 0 else at(z + d, y)
                    cs.append(put(ref, ref, ssem.at[i], rsem.at[i], dev))
            for c in cs:
                c.wait_recv()
            merged = [None, None]
            for axis, buf in ((0, xy), (1, xz)):
                part = axis ^ stage
                merged[part] = merge([buf[n, stage, q, 0:32, :] for q in range(4)])
                if extra is not None and part == 0:
                    more = total([buf[n, stage, q, 32:40, :] for q in range(4)])[0:1, 0:1]
            vals = merged
            extra = more if extra is not None else None
        return jnp.concatenate(vals, axis=0), extra

    turned = jnp.concatenate([wt_ref[...], jnp.ones((96, 128), jnp.float32)], axis=0).T
    wt = jnp.where(lane64 < 32, turned[0:64], pltpu.roll(turned[64:128], 32, 1))
    cap = cap_ref[...]
    wsum = jnp.sum(jnp.where(lane64 < 64, wt, 0.0), keepdims=True)
    csum = jnp.sum(cap, keepdims=True)
    logwt = jnp.log(wt)

    def col_first(f1, b, at, carry):
        f = column(f1, at)
        for k in range(KP):
            c = s_ref[b, :, ks(k)] + f
            m = jnp.max(c, axis=0, keepdims=True)
            tm_ref[rows_at(k, b), :] = m
            ts_ref[rows_at(k, b), :] = jnp.sum(jnp.exp(c - m), axis=0, keepdims=True)
        return carry

    f1 = rows_then_cols(0, score_block, csum, lse, lambda r: logwt - r, col_first)
    extra = slice(LANES // 2, LANES // 2 + 8)
    capacity = total([xrow[0, 0, q, extra, :] for q in range(8)])[0:1, 0:1]

    block = lax.broadcasted_iota(jnp.int32, (128, 128), 0)

    def spread_max(r, acc):
        for u in range(4):
            one = pl.ds(r * 4 + u, 1)
            acc = jnp.maximum(acc, jnp.where(block == tgt_ref[one, :], tm_ref[one, :], NEG))
        return acc

    peak = lax.fori_loop(0, 64, spread_max, jnp.full((128, 128), NEG, jnp.float32))
    peak = jnp.maximum(peak, pltpu.roll(peak, 64, 1))

    lanes = lax.broadcasted_iota(jnp.int32, (256, 128), 1)
    tgt = tgt_ref[...]
    hot = jnp.concatenate(
        [jnp.where(lanes == tgt[:, 0:1], 1.0, 0.0), jnp.where(lanes == tgt[:, 64:65], 1.0, 0.0)], axis=1
    )
    hot_t = jnp.concatenate(
        [hot[:, 0:128].T, hot[:, 128:256].T], axis=1
    ).astype(jnp.bfloat16)
    hot = hot.astype(jnp.bfloat16)

    def hot_dot(one, v):
        out = []
        for _ in range(3):
            h = v.astype(jnp.bfloat16).astype(jnp.float32)
            out.append(h)
            v = v - h
        w = jnp.concatenate(out, axis=1)
        side = (lax.broadcasted_iota(jnp.int32, (1, 384), 1) & 64) == 0
        w = jnp.concatenate([jnp.where(side, w, 0.0), jnp.where(side, 0.0, w)], axis=0)
        o = jnp.dot(one, w.astype(jnp.bfloat16), preferred_element_type=jnp.float32)
        return o[:, 0:128] + (o[:, 128:256] + o[:, 256:384])

    def spread_out(v):
        return hot_dot(hot, v)

    def collect(v):
        o = hot_dot(hot_t, v)
        return o + pltpu.roll(o, 64, 1)

    def compact(v):
        return jnp.where(left, v[0:64], v[64:128])

    def expand(c):
        r = pltpu.roll(c, 64, 1)
        return jnp.concatenate([jnp.where(left, c, r), jnp.where(left, r, c)], axis=0)

    tiles = ts_ref[...] * jnp.exp(tm_ref[...] - spread_out(peak))
    sums = collect(tiles)
    some = sums > 0.0
    col = jnp.where(some, peak + jnp.log(jnp.where(some, sums, 1.0)), NEG)
    col, weight = col_exchange(0, compact(col), wsum, lse)
    lw = jnp.log(weight)
    f1 = f1 - lw
    g1 = jnp.log(cap) - jnp.log(capacity) - (col - lw)
    amass = wt / weight
    bmass = cap / capacity

    tm_ref[...] = spread_out(expand(g1))

    def first_rows(b, at, acc):
        f = column(f1, at)
        t = None
        for k in range(KP):
            e = jnp.exp(s_ref[b, :, ks(k)] + f + tm_ref[rows_at(k, b), :])
            s_ref[b, :, ks(k)] = e
            t = e if t is None else t + e
        return jnp.where(lane64 == at, jnp.sum(t, axis=1, keepdims=True), acc)

    def cols(u, b, at, carry):
        c = column(u, at)
        for k in range(KP):
            ts_ref[rows_at(k, b), :] = jnp.sum(s_ref[b, :, ks(k)] * c, axis=0, keepdims=True)
        return carry

    u = rows_then_cols(1, first_rows, None, total, lambda r: amass / r, cols)
    v = bmass / col_exchange(1, compact(collect(ts_ref[...])), None, total)[0]

    tm_ref[...] = spread_out(expand(v))

    def rows(b, at, acc):
        t = functools.reduce(
            jnp.add, [s_ref[b, :, ks(k)] * tm_ref[rows_at(k, b), :] for k in range(KP)]
        )
        return jnp.where(lane64 == at, jnp.sum(t, axis=1, keepdims=True), acc)

    u = rows_then_cols(2, rows, None, total, lambda r: amass / r, cols)
    f = f1 + jnp.log(u)
    fout_ref[...] = jnp.concatenate([f, pltpu.roll(f, 96, 1)], axis=0).T[0:32]
    v = bmass / col_exchange(2, compact(collect(ts_ref[...])), None, total)[0]
    gout_ref[...] = g1 + jnp.log(v)

    for c in sends:
        c.wait_send()


def body(residuals, codebook, item_weight, code_capacity, pairs):
    items = residuals.shape[1]
    codes = codebook.shape[1]
    vm = pl.BlockSpec(memory_space=pltpu.VMEM)
    hbm = pl.BlockSpec(memory_space=pl.ANY)
    f32, bf16 = jnp.float32, jnp.bfloat16
    dma = pltpu.SemaphoreType.DMA
    f, g = pl.pallas_call(
        kernel,
        out_shape=[jax.ShapeDtypeStruct((32, 128), f32), jax.ShapeDtypeStruct((64, 128), f32)],
        in_specs=[hbm, hbm, vm, vm, hbm],
        out_specs=[vm, vm],
        scratch_shapes=[
            pltpu.VMEM((16, 2, 8, codes), f32),
            pltpu.VMEM((16, 16, items), f32),
            pltpu.VMEM((128, 16, 16, 128), bf16),
            pltpu.VMEM((128, 16, 16, 128), bf16),
            pltpu.VMEM((64, 128, 256), bf16),
            pltpu.VMEM((64, 64, 512), f32),
            pltpu.VMEM((16, 64), jnp.int32),
            pltpu.VMEM((128, 128), jnp.int32),
            pltpu.VMEM((256, 128), jnp.int32),
            pltpu.VMEM((64, 128), jnp.int32),
            pltpu.SMEM((64, 128), jnp.int32),
            pltpu.VMEM((256, 128), f32),
            pltpu.VMEM((256, 128), f32),
            pltpu.VMEM((3, PARTS, 8, LANES // 2 + 8, 128), f32),
            pltpu.VMEM((3, 2, 4, 40, 128), f32),
            pltpu.VMEM((3, 2, 4, 40, 128), f32),
            dma((64,)),
            dma((64,)),
            dma((8,)),
            dma((8,)),
            dma((4,)),
            dma((21 * PARTS,)),
            dma((21 * PARTS,)),
            dma((18,)),
            dma((18,)),
            dma((18,)),
            dma((18,)),
        ],
        compiler_params=pltpu.CompilerParams(
            collective_id=0, has_side_effects=True, vmem_limit_bytes=60 * 1024 * 1024
        ),
    )(
        codebook.reshape(2, 8, codes),
        residuals.reshape(2, 16, items),
        item_weight.reshape(32, 128),
        code_capacity.reshape(64, 128),
        pairs.T,
    )
    return f.reshape(items), g.reshape(codes)


def solution(mesh):
    placed = (P("code", "item"), P("item", "code"), P("item"), P("code"), P("item", "code"))
    return jax.shard_map(
        body, mesh=mesh, in_specs=placed, out_specs=(P("item"), P("code")), check_vma=False
    )
```

```python
import functools
import math

import jax
import jax.numpy as jnp
from jax import lax
from jax.experimental import pallas as pl
from jax.experimental.pallas import tpu as pltpu
from jax.sharding import PartitionSpec as P

BLOCK = 64
SLOTS = 8
KP = SLOTS // 2
NEG = -1e30
PARTS = 4
LANES = 64 // PARTS
ORDER = [(0, 0), (0, 3), (3, 0), (0, 1), (1, 0), (0, 2), (2, 0), (3, 3), (1, 3), (3, 1), (1, 1), (3, 2), (2, 3), (1, 2), (2, 1), (2, 2)]
SOFTNESS = 0.1
MESH = pl.DeviceIdType.MESH


def kernel(
    cb_ref,
    res_ref,
    wt_ref,
    cap_ref,
    pairs_ref,
    fout_ref,
    gout_ref,
    cg,
    rg,
    vh,
    vl,
    rt,
    s_ref,
    slots,
    padded,
    tgt_ref,
    ids_v,
    ids_ref,
    tm_ref,
    ts_ref,
    xrow,
    xy,
    xz,
    csend,
    crecv,
    rsend,
    rrecv,
    lsem,
    rowsend,
    rowrecv,
    ysend,
    yrecv,
    zsend,
    zrecv,
):
    item = lax.axis_index("item")
    code = lax.axis_index("code")
    z, y = item // 4, item % 4
    x, core = code // 2, code % 2
    cd = cg.shape[3]
    idv = rg.shape[2]
    width = 256
    scale = 1.0 / (SOFTNESS * math.sqrt(width))

    def at(zz, yy):
        return {"item": (zz % 4) * 4 + yy % 4, "code": code}

    def ac(cc):
        return {"item": item, "code": cc}

    bar = pltpu.get_barrier_semaphore()
    for d in range(1, 4):
        pl.semaphore_signal(bar, inc=1, device_id=at(z, y + d), device_id_type=MESH)
        pl.semaphore_signal(bar, inc=1, device_id=at(z + d, y), device_id_type=MESH)
    for d in range(1, 8):
        pl.semaphore_signal(bar, inc=1, device_id=ac((code + d) % 8), device_id_type=MESH)

    lane = lax.broadcasted_iota(jnp.int32, (1, 128), 1)
    left = lane < 64
    lane64 = lax.broadcasted_iota(jnp.int32, (64, 128), 1)
    sc = pltpu.make_async_copy(pairs_ref, slots, lsem.at[3])
    sc.start()
    padded[...] = jnp.full((128, 128), -1, jnp.int32)
    sc.wait()
    padded[0:16, 0:64] = slots[...]
    named = padded[...].T[0:64]
    live = jnp.where(named >= 0, 1, 0)
    count = live
    for sh in (1, 2, 4, 8):
        count = count + jnp.where(lane64 >= sh, pltpu.roll(count, sh, 1), 0)
    count = live * count
    picked = []
    ids = jnp.zeros((64, 128), jnp.int32)
    for k in range(SLOTS):
        one = jnp.max(jnp.where(count == k + 1, named, -1), axis=1, keepdims=True)
        ids = jnp.where(lane64 == k, jnp.maximum(one, 0) ^ (k & 1), ids)
        picked.append(jnp.where(one < 0, -1, (one >> 1) + (one & 1) * 64))
    for k in range(KP):
        tgt_ref[k * 64 : k * 64 + 64, :] = jnp.where(left, picked[2 * k], picked[2 * k + 1])
    ids_v[...] = ids
    idc = pltpu.make_async_copy(ids_v, ids_ref, lsem.at[3])
    idc.start()
    idc.wait()
    pl.semaphore_wait(bar, 13)

    half = cd // 2
    sends = []

    def put(src, dst, ss, rs, dev):
        c = pltpu.make_async_remote_copy(
            src_ref=src, dst_ref=dst, send_sem=ss, recv_sem=rs, device_id=dev, device_id_type=MESH
        )
        c.start()
        sends.append(c)
        return c

    def place(h, p, s):
        zz, yy = (s, p) if h == 0 else (p, s)
        return (zz % 4) * 4 + yy % 4

    def where_to(h, p, s):
        zz, yy = (s, p) if h == 0 else (p, s)
        return at(zz, yy)

    pos = [(y, z), (z, y)]
    cnt = [0]

    def cput(h, src_ps, c, to, own=False):
        i = cnt[0]
        cnt[0] += 1
        col = pl.ds(c * half, half)
        dst = cg.at[place(h, *src_ps), h, :, col]
        src = cb_ref.at[h, :, col] if own else dst
        return put(src, dst, csend.at[i], crecv.at[i], where_to(h, *to))

    def first(d):
        return 0 if d > 0 else 1

    dirs = [(h, d) for d in (1, -1) for h in range(2)]
    prim, sec = {}, {}
    locals_ = []
    for turn in range(2):
        for h, d in dirs:
            p, s = pos[h]
            c = first(d) ^ turn
            prim[h, d, c] = cput(h, (p, s), c, (p + d, s), True)
        for h, d in dirs:
            p, s = pos[h]
            c = first(d) ^ turn
            sec[h, 0, d, c] = cput(h, (p, s), c, (p, s + d), True)
    for h in range(2):
        lc = pltpu.make_async_copy(cb_ref.at[h], cg.at[item, h], lsem.at[h])
        lc.start()
        locals_.append(lc)

    rhalf = idv // 2
    rcnt = [0]

    def rdev(xx):
        return (xx % 4) * 2 + core

    def rput(xx, cols, to, own=False):
        i = rcnt[0]
        rcnt[0] += 1
        d = rdev(xx)
        if cols is None:
            dst = rg.at[pl.ds(2 * d, 2)]
        else:
            dst = rg.at[pl.ds(2 * d, 2), :, pl.ds(cols * rhalf, rhalf)]
        return put(res_ref if own else dst, dst, rsend.at[i], rrecv.at[i], ac(to))

    other = x * 2 + (1 - core)
    rp = {}
    rp[1] = rput(x, None, rdev(x + 1), True)
    rp[-1] = rput(x, None, rdev(x - 1), True)
    rc = [rput(x, None, other, True)]
    lc = pltpu.make_async_copy(res_ref, rg.at[pl.ds(2 * code, 2)], lsem.at[2])
    lc.start()
    locals_.append(lc)

    UN = 8
    leftw = lax.broadcasted_iota(jnp.int32, (width // 2, 128), 1) < 64

    def rows_at(k, b):
        return pl.ds(k * 64 + b, 1)

    def column(f, at):
        return jnp.sum(jnp.where(lane64 == at, f, 0.0), axis=1, keepdims=True)

    def ks(k):
        return slice(k * 128, k * 128 + 128)

    def blocks(part, body, init, un=UN):
        low = part * LANES

        def step(j, acc):
            for r in range(un):
                i = j * un + r
                acc = body(2 * (low % 32 + i) + low // 32, low + i, acc)
            return acc

        return lax.fori_loop(0, LANES // un, step, init)

    def score_part(b, part):
        r8 = pl.ds(part * 8, 8)
        wh, wl = [], []
        for k in range(KP):
            i0 = ids_ref[b, 2 * k]
            i1 = ids_ref[b, 2 * k + 1]
            for ref, out in ((vh, wh), (vl, wl)):
                one = ref[i0, r8].reshape(width // 2, 128)
                two = ref[i1, r8].reshape(width // 2, 128)
                out.append(jnp.where(leftw, one, two))
        a = rt[b, :, part * 128 : part * 128 + 128]
        ss = []
        for k in range(0, KP, 2):
            d1 = jnp.dot(a, jnp.concatenate(wh[k : k + 2], axis=1), preferred_element_type=jnp.float32)
            d2 = jnp.dot(
                a[0:64], jnp.concatenate(wl[k : k + 2], axis=1), preferred_element_type=jnp.float32
            )
            t = d1[0:64] + (d1[64:128] + d2)
            ss += [t[:, 0:128], t[:, 128:256]]
        return ss

    def score_half(g):
        for r in range(8):
            b = g * 8 + r
            for k, t in enumerate(score_part(b, 0)):
                s_ref[b, :, ks(k)] = t

    tasks = []
    parts = {}
    ready = [0]
    per = [1]

    def split_items(c, carry):
        col = pl.ds(pl.multiple_of(c * 128, 128), 128)
        v = jnp.concatenate([rg[source(k), :, col] for k in ORDER], axis=0).T * scale
        hi = v.astype(jnp.bfloat16)
        lo = (v - hi.astype(jnp.float32)).astype(jnp.bfloat16)
        for b in range(2):
            rt[2 * c + b, 0:64, :] = hi[b * 64 : b * 64 + 64]
            rt[2 * c + b, 64:128, :] = lo[b * 64 : b * 64 + 64]
        return carry

    def source(key):
        return ((z + key[1]) % 4) * 4 + (y + key[0]) % 4

    def split_codes(d, rank):
        def step(j, carry):
            for r in range(8):
                q = j * 8 + r
                col = pl.ds(pl.multiple_of(q * 128, 128), 128)
                v = cg[d, :, :, col].reshape(16, 128)
                for b, t in ((0, v), (1, pltpu.roll(v, 64, 1))):
                    hi = t.astype(jnp.bfloat16)
                    vh[2 * q + b, rank] = hi
                    vl[2 * q + b, rank] = (t - hi.astype(jnp.float32)).astype(jnp.bfloat16)
            return carry

        lax.fori_loop(0, cd // 1024, step, 0)

    def got(h, op, os, share):
        dy, dz = ((op, os) if h == 0 else (os, op))
        key = dy % 4, dz % 4
        parts[key] = parts.get(key, 0) + share
        if parts[key] == 4:
            r = ready[0]
            ready[0] += 1
            assert ORDER[r] == key
            tasks.append(lambda: split_codes(source(key), r))
            if r == 7:
                for g in range(8):
                    tasks.append(lambda g=g: score_half(g))

    def work(n):
        for _ in range(min(n, len(tasks))):
            tasks.pop(0)()

    ph, sh = {}, {}
    offs = {0: 0, 1: -1, -1: 1, 2: 2}

    def pass_on(h, k, c):
        p, s = pos[h]
        for d in (1, -1) if c == 0 else (-1, 1):
            sec[h, k, d, c] = cput(h, (p + offs[k], s), c, (p, s + d))

    def forward(k):
        for h, d in dirs:
            p, s = pos[h]
            c = first(d)
            if k in (1, -1):
                work(1)
            sec[h, k, d, c].wait_recv()
            sh[h, k, d] = cput(h, (p + offs[k], s - d), c, (p, s + d))
            got(h, offs[k], -d, 1)

    def take(k, turn):
        for h, d in dirs:
            work(per[0])
            if turn:
                sec[h, k, d, 1 - first(d)].wait_recv()
                got(h, offs[k], -d, 1)
            else:
                sh[h, k, d].wait_recv()
                got(h, offs[k], 2, 1)

    for h, d in dirs:
        p, s = pos[h]
        c = first(d)
        prim[h, d, c].wait_recv()
        ph[h, d] = cput(h, (p - d, s), c, (p + d, s))
        pass_on(h, d, c)
        got(h, -d, 0, 1)
    forward(0)
    for h, d in dirs:
        c = 1 - first(d)
        prim[h, d, c].wait_recv()
        pass_on(h, d, c)
        got(h, -d, 0, 1)
    for d in (1, -1):
        rp[d].wait_recv()
        rp[2 * d] = rput(x - d, 0 if d > 0 else 1, rdev(x + d))
        rc.append(rput(x - d, None, other))
    for h, d in dirs:
        ph[h, d].wait_recv()
        pass_on(h, 2, first(d))
        got(h, 2, 0, 1)
    for c in locals_:
        c.wait()
    for h in range(2):
        got(h, 0, 0, 2)
    take(0, 1)
    rp[2].wait_recv()
    rp[-2].wait_recv()
    rc.append(rput(x + 2, None, other))
    forward(1)
    forward(-1)
    for c in rc:
        c.wait_recv()
    for g in range(8):
        n = idv // 128 // 8
        tasks.append(lambda g=g, n=n: lax.fori_loop(g * n, g * n + n, split_items, 0))
    take(0, 0)
    take(1, 1)
    take(-1, 1)
    forward(2)
    per[0] = 2
    take(2, 1)
    for k in (1, -1, 2):
        take(k, 0)
    work(len(tasks))

    def score_block(b, at, acc):
        ss = score_part(b, 1)
        for k in range(KP):
            ss[k] = jnp.where(tgt_ref[rows_at(k, b), :] >= 0, ss[k] + s_ref[b, :, ks(k)], NEG)
            s_ref[b, :, ks(k)] = ss[k]
        m = jnp.max(functools.reduce(jnp.maximum, ss), axis=1, keepdims=True)
        t = functools.reduce(jnp.add, [jnp.exp(s - m) for s in ss])
        t = jnp.sum(t, axis=1, keepdims=True)
        return jnp.where(lane64 == at, m + jnp.log(t), acc)

    def group(g):
        return slice(g * LANES // 2, g * LANES // 2 + LANES // 2)

    def pack(part, r):
        out = r[group(0)] if part == 0 else pltpu.roll(r[group(0)], (-part * LANES) % 128, 1)
        for g in range(1, 128 // LANES):
            shift = ((g - part) * LANES) % 128
            one = pltpu.roll(r[group(g)], shift, 1) if shift else r[group(g)]
            out = jnp.where(lane < g * LANES, out, one)
        return out

    def unpack(part, m):
        out = []
        for g in range(128 // LANES):
            shift = ((part - g) * LANES) % 128
            out.append(pltpu.roll(m, shift, 1) if shift else m)
        return jnp.concatenate(out, axis=0)

    def of_part(part):
        return (lane64 >= part * LANES) & (lane64 < part * LANES + LANES)

    def lse(parts):
        m = functools.reduce(jnp.maximum, parts)
        t = functools.reduce(jnp.add, [jnp.exp(q - m) for q in parts])
        return m + jnp.log(t)

    def total(parts):
        return functools.reduce(jnp.add, parts)

    def row_send(n, part, r, extra=None):
        size = LANES // 2
        xrow[n, part, code, 0:size, :] = pack(part, r)
        if extra is not None:
            xrow[n, part, code, size : size + 8, :] = jnp.broadcast_to(extra, (8, 128))
            size += 8
        cs = []
        for d in range(1, 8):
            ref = xrow.at[n, part, code, pl.ds(0, size), :]
            i = (n * PARTS + part) * 7 + d - 1
            cs.append(put(ref, ref, rowsend.at[i], rowrecv.at[i], ac((code + d) % 8)))
        return cs

    def row_receive(n, part, cs, merge):
        for c in cs:
            c.wait_recv()
        return unpack(part, merge([xrow[n, part, q, 0 : LANES // 2, :] for q in range(8)]))

    def rows_then_cols(n, row_body, extra, merge, finish, col_body):
        sent = []
        for part in range(PARTS):
            r = blocks(part, row_body, jnp.ones((64, 128), jnp.float32))
            sent.append(row_send(n, part, r, extra if part == 0 else None))
        out = jnp.zeros((64, 128), jnp.float32)
        for part in range(PARTS):
            r = row_receive(n, part, sent[part], merge)
            out = jnp.where(of_part(part), finish(r), out)
            blocks(part, functools.partial(col_body, out), 0)
        return out

    def col_exchange(n, val, extra, merge):
        vals = [val[0:32], val[32:64]]
        for stage in range(2):
            cs = []
            for axis, buf, me, ssem, rsem in ((0, xy, y, ysend, yrecv), (1, xz, z, zsend, zrecv)):
                part = axis ^ stage
                size = 32
                buf[n, stage, me, 0:32, :] = vals[part]
                if extra is not None and part == 0:
                    buf[n, stage, me, 32:40, :] = jnp.broadcast_to(extra, (8, 128))
                    size = 40
                for d in (2, 1, 3):
                    ref = buf.at[n, stage, me, pl.ds(0, size), :]
                    i = (n * 2 + stage) * 3 + d - 1
                    dev = at(z, y + d) if axis == 0 else at(z + d, y)
                    cs.append(put(ref, ref, ssem.at[i], rsem.at[i], dev))
            for c in cs:
                c.wait_recv()
            merged = [None, None]
            for axis, buf in ((0, xy), (1, xz)):
                part = axis ^ stage
                merged[part] = merge([buf[n, stage, q, 0:32, :] for q in range(4)])
                if extra is not None and part == 0:
                    more = total([buf[n, stage, q, 32:40, :] for q in range(4)])[0:1, 0:1]
            vals = merged
            extra = more if extra is not None else None
        return jnp.concatenate(vals, axis=0), extra

    turned = jnp.concatenate([wt_ref[...], jnp.ones((96, 128), jnp.float32)], axis=0).T
    wt = jnp.where(lane64 < 32, turned[0:64], pltpu.roll(turned[64:128], 32, 1))
    cap = cap_ref[...]
    wsum = jnp.sum(jnp.where(lane64 < 64, wt, 0.0), keepdims=True)
    csum = jnp.sum(cap, keepdims=True)
    logwt = jnp.log(wt)

    def col_first(f1, b, at, carry):
        f = column(f1, at)
        for k in range(KP):
            c = s_ref[b, :, ks(k)] + f
            m = jnp.max(c, axis=0, keepdims=True)
            tm_ref[rows_at(k, b), :] = m
            ts_ref[rows_at(k, b), :] = jnp.sum(jnp.exp(c - m), axis=0, keepdims=True)
        return carry

    f1 = rows_then_cols(0, score_block, csum, lse, lambda r: logwt - r, col_first)
    extra = slice(LANES // 2, LANES // 2 + 8)
    capacity = total([xrow[0, 0, q, extra, :] for q in range(8)])[0:1, 0:1]

    block = lax.broadcasted_iota(jnp.int32, (128, 128), 0)

    def spread_max(r, acc):
        for u in range(4):
            one = pl.ds(r * 4 + u, 1)
            acc = jnp.maximum(acc, jnp.where(block == tgt_ref[one, :], tm_ref[one, :], NEG))
        return acc

    peak = lax.fori_loop(0, 64, spread_max, jnp.full((128, 128), NEG, jnp.float32))
    peak = jnp.maximum(peak, pltpu.roll(peak, 64, 1))

    lanes = lax.broadcasted_iota(jnp.int32, (256, 128), 1)
    tgt = tgt_ref[...]
    hot = jnp.concatenate(
        [jnp.where(lanes == tgt[:, 0:1], 1.0, 0.0), jnp.where(lanes == tgt[:, 64:65], 1.0, 0.0)], axis=1
    )
    hot_t = jnp.concatenate(
        [hot[:, 0:128].T, hot[:, 128:256].T], axis=1
    ).astype(jnp.bfloat16)
    hot = hot.astype(jnp.bfloat16)

    def hot_dot(one, v):
        out = []
        for _ in range(3):
            h = v.astype(jnp.bfloat16).astype(jnp.float32)
            out.append(h)
            v = v - h
        w = jnp.concatenate(out, axis=1)
        side = (lax.broadcasted_iota(jnp.int32, (1, 384), 1) & 64) == 0
        w = jnp.concatenate([jnp.where(side, w, 0.0), jnp.where(side, 0.0, w)], axis=0)
        o = jnp.dot(one, w.astype(jnp.bfloat16), preferred_element_type=jnp.float32)
        return o[:, 0:128] + (o[:, 128:256] + o[:, 256:384])

    def spread_out(v):
        return hot_dot(hot, v)

    def collect(v):
        o = hot_dot(hot_t, v)
        return o + pltpu.roll(o, 64, 1)

    def compact(v):
        return jnp.where(left, v[0:64], v[64:128])

    def expand(c):
        r = pltpu.roll(c, 64, 1)
        return jnp.concatenate([jnp.where(left, c, r), jnp.where(left, r, c)], axis=0)

    tiles = ts_ref[...] * jnp.exp(tm_ref[...] - spread_out(peak))
    sums = collect(tiles)
    some = sums > 0.0
    col = jnp.where(some, peak + jnp.log(jnp.where(some, sums, 1.0)), NEG)
    col, weight = col_exchange(0, compact(col), wsum, lse)
    lw = jnp.log(weight)
    f1 = f1 - lw
    g1 = jnp.log(cap) - jnp.log(capacity) - (col - lw)
    amass = wt / weight
    bmass = cap / capacity

    tm_ref[...] = spread_out(expand(g1))

    def first_rows(b, at, acc):
        f = column(f1, at)
        t = None
        for k in range(KP):
            e = jnp.exp(s_ref[b, :, ks(k)] + f + tm_ref[rows_at(k, b), :])
            s_ref[b, :, ks(k)] = e
            t = e if t is None else t + e
        return jnp.where(lane64 == at, jnp.sum(t, axis=1, keepdims=True), acc)

    def cols(u, b, at, carry):
        c = column(u, at)
        for k in range(KP):
            ts_ref[rows_at(k, b), :] = jnp.sum(s_ref[b, :, ks(k)] * c, axis=0, keepdims=True)
        return carry

    u = rows_then_cols(1, first_rows, None, total, lambda r: amass / r, cols)
    v = bmass / col_exchange(1, compact(collect(ts_ref[...])), None, total)[0]

    tm_ref[...] = spread_out(expand(v))

    def rows(b, at, acc):
        t = functools.reduce(
            jnp.add, [s_ref[b, :, ks(k)] * tm_ref[rows_at(k, b), :] for k in range(KP)]
        )
        return jnp.where(lane64 == at, jnp.sum(t, axis=1, keepdims=True), acc)

    u = rows_then_cols(2, rows, None, total, lambda r: amass / r, cols)
    f = f1 + jnp.log(u)
    fout_ref[...] = jnp.concatenate([f, pltpu.roll(f, 96, 1)], axis=0).T[0:32]
    v = bmass / col_exchange(2, compact(collect(ts_ref[...])), None, total)[0]
    gout_ref[...] = g1 + jnp.log(v)

    for c in sends:
        c.wait_send()


def body(residuals, codebook, item_weight, code_capacity, pairs):
    items = residuals.shape[1]
    codes = codebook.shape[1]
    vm = pl.BlockSpec(memory_space=pltpu.VMEM)
    hbm = pl.BlockSpec(memory_space=pl.ANY)
    f32, bf16 = jnp.float32, jnp.bfloat16
    dma = pltpu.SemaphoreType.DMA
    f, g = pl.pallas_call(
        kernel,
        out_shape=[jax.ShapeDtypeStruct((32, 128), f32), jax.ShapeDtypeStruct((64, 128), f32)],
        in_specs=[hbm, hbm, vm, vm, hbm],
        out_specs=[vm, vm],
        scratch_shapes=[
            pltpu.VMEM((16, 2, 8, codes), f32),
            pltpu.VMEM((16, 16, items), f32),
            pltpu.VMEM((128, 16, 16, 128), bf16),
            pltpu.VMEM((128, 16, 16, 128), bf16),
            pltpu.VMEM((64, 128, 256), bf16),
            pltpu.VMEM((64, 64, 512), f32),
            pltpu.VMEM((16, 64), jnp.int32),
            pltpu.VMEM((128, 128), jnp.int32),
            pltpu.VMEM((256, 128), jnp.int32),
            pltpu.VMEM((64, 128), jnp.int32),
            pltpu.SMEM((64, 128), jnp.int32),
            pltpu.VMEM((256, 128), f32),
            pltpu.VMEM((256, 128), f32),
            pltpu.VMEM((3, PARTS, 8, LANES // 2 + 8, 128), f32),
            pltpu.VMEM((3, 2, 4, 40, 128), f32),
            pltpu.VMEM((3, 2, 4, 40, 128), f32),
            dma((64,)),
            dma((64,)),
            dma((8,)),
            dma((8,)),
            dma((4,)),
            dma((21 * PARTS,)),
            dma((21 * PARTS,)),
            dma((18,)),
            dma((18,)),
            dma((18,)),
            dma((18,)),
        ],
        compiler_params=pltpu.CompilerParams(
            collective_id=0, has_side_effects=True, vmem_limit_bytes=60 * 1024 * 1024
        ),
    )(
        codebook.reshape(2, 8, codes),
        residuals.reshape(2, 16, items),
        item_weight.reshape(32, 128),
        code_capacity.reshape(64, 128),
        pairs.T,
    )
    return f.reshape(items), g.reshape(codes)


def solution(mesh):
    placed = (P("code", "item"), P("item", "code"), P("item"), P("code"), P("item", "code"))
    return jax.shard_map(
        body, mesh=mesh, in_specs=placed, out_specs=(P("item"), P("code")), check_vma=False
    )
```

```python
import functools
import math

import jax
import jax.numpy as jnp
from jax import lax
from jax.experimental import pallas as pl
from jax.experimental.pallas import tpu as pltpu
from jax.sharding import PartitionSpec as P

BLOCK = 64
SLOTS = 8
KP = SLOTS // 2
NEG = -1e30
PARTS = 4
LANES = 64 // PARTS
ORDER = [(0, 0), (0, 3), (3, 0), (0, 1), (1, 0), (0, 2), (2, 0), (3, 3), (1, 3), (3, 1), (1, 1), (3, 2), (2, 3), (1, 2), (2, 1), (2, 2)]
SOFTNESS = 0.1
MESH = pl.DeviceIdType.MESH


def kernel(
    cb_ref,
    res_ref,
    wt_ref,
    cap_ref,
    pairs_ref,
    fout_ref,
    gout_ref,
    cg,
    rg,
    vh,
    vl,
    rt,
    s_ref,
    slots,
    padded,
    tgt_ref,
    ids_v,
    ids_ref,
    tm_ref,
    ts_ref,
    xrow,
    xy,
    xz,
    csend,
    crecv,
    rsend,
    rrecv,
    lsem,
    rowsend,
    rowrecv,
    ysend,
    yrecv,
    zsend,
    zrecv,
):
    item = lax.axis_index("item")
    code = lax.axis_index("code")
    z, y = item // 4, item % 4
    x, core = code // 2, code % 2
    cd = cg.shape[3]
    idv = rg.shape[2]
    width = 256
    scale = 1.0 / (SOFTNESS * math.sqrt(width))

    def at(zz, yy):
        return {"item": (zz % 4) * 4 + yy % 4, "code": code}

    def ac(cc):
        return {"item": item, "code": cc}

    bar = pltpu.get_barrier_semaphore()
    for d in range(1, 4):
        pl.semaphore_signal(bar, inc=1, device_id=at(z, y + d), device_id_type=MESH)
        pl.semaphore_signal(bar, inc=1, device_id=at(z + d, y), device_id_type=MESH)
    for d in range(1, 8):
        pl.semaphore_signal(bar, inc=1, device_id=ac((code + d) % 8), device_id_type=MESH)

    lane = lax.broadcasted_iota(jnp.int32, (1, 128), 1)
    left = lane < 64
    lane64 = lax.broadcasted_iota(jnp.int32, (64, 128), 1)
    sc = pltpu.make_async_copy(pairs_ref, slots, lsem.at[3])
    sc.start()
    padded[...] = jnp.full((128, 128), -1, jnp.int32)
    sc.wait()
    padded[0:16, 0:64] = slots[...]
    named = padded[...].T[0:64]
    live = jnp.where(named >= 0, 1, 0)
    count = live
    for sh in (1, 2, 4, 8):
        count = count + jnp.where(lane64 >= sh, pltpu.roll(count, sh, 1), 0)
    count = live * count
    picked = []
    ids = jnp.zeros((64, 128), jnp.int32)
    for k in range(SLOTS):
        one = jnp.max(jnp.where(count == k + 1, named, -1), axis=1, keepdims=True)
        ids = jnp.where(lane64 == k, jnp.maximum(one, 0) ^ (k & 1), ids)
        picked.append(jnp.where(one < 0, -1, (one >> 1) + (one & 1) * 64))
    for k in range(KP):
        tgt_ref[k * 64 : k * 64 + 64, :] = jnp.where(left, picked[2 * k], picked[2 * k + 1])
    ids_v[...] = ids
    idc = pltpu.make_async_copy(ids_v, ids_ref, lsem.at[3])
    idc.start()
    idc.wait()
    pl.semaphore_wait(bar, 13)

    half = cd // 2
    sends = []

    def put(src, dst, ss, rs, dev):
        c = pltpu.make_async_remote_copy(
            src_ref=src, dst_ref=dst, send_sem=ss, recv_sem=rs, device_id=dev, device_id_type=MESH
        )
        c.start()
        sends.append(c)
        return c

    def place(h, p, s):
        zz, yy = (s, p) if h == 0 else (p, s)
        return (zz % 4) * 4 + yy % 4

    def where_to(h, p, s):
        zz, yy = (s, p) if h == 0 else (p, s)
        return at(zz, yy)

    pos = [(y, z), (z, y)]
    cnt = [0]

    def cput(h, src_ps, c, to, own=False):
        i = cnt[0]
        cnt[0] += 1
        col = pl.ds(c * half, half)
        dst = cg.at[place(h, *src_ps), h, :, col]
        src = cb_ref.at[h, :, col] if own else dst
        return put(src, dst, csend.at[i], crecv.at[i], where_to(h, *to))

    def first(d):
        return 0 if d > 0 else 1

    dirs = [(h, d) for d in (1, -1) for h in range(2)]
    prim, sec = {}, {}
    locals_ = []
    for turn in range(2):
        for h, d in dirs:
            p, s = pos[h]
            c = first(d) ^ turn
            prim[h, d, c] = cput(h, (p, s), c, (p + d, s), True)
        for h, d in dirs:
            p, s = pos[h]
            c = first(d) ^ turn
            sec[h, 0, d, c] = cput(h, (p, s), c, (p, s + d), True)
    for h in range(2):
        lc = pltpu.make_async_copy(cb_ref.at[h], cg.at[item, h], lsem.at[h])
        lc.start()
        locals_.append(lc)

    rhalf = idv // 2
    rcnt = [0]

    def rdev(xx):
        return (xx % 4) * 2 + core

    def rput(xx, cols, to, own=False):
        i = rcnt[0]
        rcnt[0] += 1
        d = rdev(xx)
        if cols is None:
            dst = rg.at[pl.ds(2 * d, 2)]
        else:
            dst = rg.at[pl.ds(2 * d, 2), :, pl.ds(cols * rhalf, rhalf)]
        return put(res_ref if own else dst, dst, rsend.at[i], rrecv.at[i], ac(to))

    other = x * 2 + (1 - core)
    rp = {}
    rp[1] = rput(x, None, rdev(x + 1), True)
    rp[-1] = rput(x, None, rdev(x - 1), True)
    rc = [rput(x, None, other, True)]
    lc = pltpu.make_async_copy(res_ref, rg.at[pl.ds(2 * code, 2)], lsem.at[2])
    lc.start()
    locals_.append(lc)

    UN = 8
    leftw = lax.broadcasted_iota(jnp.int32, (width // 2, 128), 1) < 64

    def rows_at(k, b):
        return pl.ds(k * 64 + b, 1)

    def column(f, at):
        return jnp.sum(jnp.where(lane64 == at, f, 0.0), axis=1, keepdims=True)

    def ks(k):
        return slice(k * 128, k * 128 + 128)

    def blocks(part, body, init, un=UN):
        low = part * LANES

        def step(j, acc):
            for r in range(un):
                i = j * un + r
                acc = body(2 * (low % 32 + i) + low // 32, low + i, acc)
            return acc

        return lax.fori_loop(0, LANES // un, step, init)

    def score_part(b, part):
        r8 = pl.ds(part * 8, 8)
        wh, wl = [], []
        for k in range(KP):
            i0 = ids_ref[b, 2 * k]
            i1 = ids_ref[b, 2 * k + 1]
            for ref, out in ((vh, wh), (vl, wl)):
                one = ref[i0, r8].reshape(width // 2, 128)
                two = ref[i1, r8].reshape(width // 2, 128)
                out.append(jnp.where(leftw, one, two))
        a = rt[b, :, part * 128 : part * 128 + 128]
        ss = []
        for k in range(0, KP, 2):
            d1 = jnp.dot(a, jnp.concatenate(wh[k : k + 2], axis=1), preferred_element_type=jnp.float32)
            d2 = jnp.dot(
                a[0:64], jnp.concatenate(wl[k : k + 2], axis=1), preferred_element_type=jnp.float32
            )
            t = d1[0:64] + (d1[64:128] + d2)
            ss += [t[:, 0:128], t[:, 128:256]]
        return ss

    def score_half(g):
        for r in range(8):
            b = g * 8 + r
            for k, t in enumerate(score_part(b, 0)):
                s_ref[b, :, ks(k)] = t

    tasks = []
    parts = {}
    ready = [0]
    per = [1]

    def split_items(c, carry):
        col = pl.ds(pl.multiple_of(c * 128, 128), 128)
        v = jnp.concatenate([rg[source(k), :, col] for k in ORDER], axis=0).T * scale
        hi = v.astype(jnp.bfloat16)
        lo = (v - hi.astype(jnp.float32)).astype(jnp.bfloat16)
        for b in range(2):
            rt[2 * c + b, 0:64, :] = hi[b * 64 : b * 64 + 64]
            rt[2 * c + b, 64:128, :] = lo[b * 64 : b * 64 + 64]
        return carry

    def source(key):
        return ((z + key[1]) % 4) * 4 + (y + key[0]) % 4

    def split_codes(d, rank):
        def step(j, carry):
            for r in range(8):
                q = j * 8 + r
                col = pl.ds(pl.multiple_of(q * 128, 128), 128)
                v = cg[d, :, :, col].reshape(16, 128)
                for b, t in ((0, v), (1, pltpu.roll(v, 64, 1))):
                    hi = t.astype(jnp.bfloat16)
                    vh[2 * q + b, rank] = hi
                    vl[2 * q + b, rank] = (t - hi.astype(jnp.float32)).astype(jnp.bfloat16)
            return carry

        lax.fori_loop(0, cd // 1024, step, 0)

    def got(h, op, os, share):
        dy, dz = ((op, os) if h == 0 else (os, op))
        key = dy % 4, dz % 4
        parts[key] = parts.get(key, 0) + share
        if parts[key] == 4:
            r = ready[0]
            ready[0] += 1
            assert ORDER[r] == key
            tasks.append(lambda: split_codes(source(key), r))
            if r == 7:
                for g in range(8):
                    tasks.append(lambda g=g: score_half(g))

    def work(n):
        for _ in range(min(n, len(tasks))):
            tasks.pop(0)()

    ph, sh = {}, {}
    offs = {0: 0, 1: -1, -1: 1, 2: 2}

    def pass_on(h, k, c):
        p, s = pos[h]
        for d in (1, -1) if c == 0 else (-1, 1):
            sec[h, k, d, c] = cput(h, (p + offs[k], s), c, (p, s + d))

    def forward(k):
        for h, d in dirs:
            p, s = pos[h]
            c = first(d)
            if k in (1, -1):
                work(1)
            sec[h, k, d, c].wait_recv()
            sh[h, k, d] = cput(h, (p + offs[k], s - d), c, (p, s + d))
            got(h, offs[k], -d, 1)

    def take(k, turn):
        for h, d in dirs:
            work(per[0])
            if turn:
                sec[h, k, d, 1 - first(d)].wait_recv()
                got(h, offs[k], -d, 1)
            else:
                sh[h, k, d].wait_recv()
                got(h, offs[k], 2, 1)

    for h, d in dirs:
        p, s = pos[h]
        c = first(d)
        prim[h, d, c].wait_recv()
        ph[h, d] = cput(h, (p - d, s), c, (p + d, s))
        pass_on(h, d, c)
        got(h, -d, 0, 1)
    forward(0)
    for h, d in dirs:
        c = 1 - first(d)
        prim[h, d, c].wait_recv()
        pass_on(h, d, c)
        got(h, -d, 0, 1)
    for d in (1, -1):
        rp[d].wait_recv()
        rp[2 * d] = rput(x - d, 0 if d > 0 else 1, rdev(x + d))
        rc.append(rput(x - d, None, other))
    for h, d in dirs:
        ph[h, d].wait_recv()
        pass_on(h, 2, first(d))
        got(h, 2, 0, 1)
    for c in locals_:
        c.wait()
    for h in range(2):
        got(h, 0, 0, 2)
    take(0, 1)
    rp[2].wait_recv()
    rp[-2].wait_recv()
    rc.append(rput(x + 2, None, other))
    forward(1)
    forward(-1)
    for c in rc:
        c.wait_recv()
    for g in range(8):
        n = idv // 128 // 8
        tasks.append(lambda g=g, n=n: lax.fori_loop(g * n, g * n + n, split_items, 0))
    take(0, 0)
    take(1, 1)
    take(-1, 1)
    forward(2)
    per[0] = 2
    take(2, 1)
    for k in (1, -1, 2):
        take(k, 0)
    work(len(tasks))

    def score_block(b, at, acc):
        ss = score_part(b, 1)
        for k in range(KP):
            ss[k] = jnp.where(tgt_ref[rows_at(k, b), :] >= 0, ss[k] + s_ref[b, :, ks(k)], NEG)
            s_ref[b, :, ks(k)] = ss[k]
        m = jnp.max(functools.reduce(jnp.maximum, ss), axis=1, keepdims=True)
        t = functools.reduce(jnp.add, [jnp.exp(s - m) for s in ss])
        t = jnp.sum(t, axis=1, keepdims=True)
        return jnp.where(lane64 == at, m + jnp.log(t), acc)

    def group(g):
        return slice(g * LANES // 2, g * LANES // 2 + LANES // 2)

    def pack(part, r):
        out = r[group(0)] if part == 0 else pltpu.roll(r[group(0)], (-part * LANES) % 128, 1)
        for g in range(1, 128 // LANES):
            shift = ((g - part) * LANES) % 128
            one = pltpu.roll(r[group(g)], shift, 1) if shift else r[group(g)]
            out = jnp.where(lane < g * LANES, out, one)
        return out

    def unpack(part, m):
        out = []
        for g in range(128 // LANES):
            shift = ((part - g) * LANES) % 128
            out.append(pltpu.roll(m, shift, 1) if shift else m)
        return jnp.concatenate(out, axis=0)

    def of_part(part):
        return (lane64 >= part * LANES) & (lane64 < part * LANES + LANES)

    def lse(parts):
        m = functools.reduce(jnp.maximum, parts)
        t = functools.reduce(jnp.add, [jnp.exp(q - m) for q in parts])
        return m + jnp.log(t)

    def total(parts):
        return functools.reduce(jnp.add, parts)

    def row_send(n, part, r, extra=None):
        size = LANES // 2
        xrow[n, part, code, 0:size, :] = pack(part, r)
        if extra is not None:
            xrow[n, part, code, size : size + 8, :] = jnp.broadcast_to(extra, (8, 128))
            size += 8
        cs = []
        for d in (4, 3, 5, 2, 6, 1, 7):
            ref = xrow.at[n, part, code, pl.ds(0, size), :]
            i = (n * PARTS + part) * 7 + d - 1
            cs.append(put(ref, ref, rowsend.at[i], rowrecv.at[i], ac((code + d) % 8)))
        return cs

    def row_receive(n, part, cs, merge):
        for c in cs:
            c.wait_recv()
        return unpack(part, merge([xrow[n, part, q, 0 : LANES // 2, :] for q in range(8)]))

    def rows_then_cols(n, row_body, extra, merge, finish, col_body):
        sent = []
        for part in range(PARTS):
            r = blocks(part, row_body, jnp.ones((64, 128), jnp.float32))
            sent.append(row_send(n, part, r, extra if part == 0 else None))
        out = jnp.zeros((64, 128), jnp.float32)
        for part in range(PARTS):
            r = row_receive(n, part, sent[part], merge)
            out = jnp.where(of_part(part), finish(r), out)
            blocks(part, functools.partial(col_body, out), 0)
        return out

    def col_exchange(n, val, extra, merge):
        vals = [val[0:32], val[32:64]]
        for stage in range(2):
            cs = []
            for axis, buf, me, ssem, rsem in ((0, xy, y, ysend, yrecv), (1, xz, z, zsend, zrecv)):
                part = axis ^ stage
                size = 32
                buf[n, stage, me, 0:32, :] = vals[part]
                if extra is not None and part == 0:
                    buf[n, stage, me, 32:40, :] = jnp.broadcast_to(extra, (8, 128))
                    size = 40
                for d in (2, 1, 3):
                    ref = buf.at[n, stage, me, pl.ds(0, size), :]
                    i = (n * 2 + stage) * 3 + d - 1
                    dev = at(z, y + d) if axis == 0 else at(z + d, y)
                    cs.append(put(ref, ref, ssem.at[i], rsem.at[i], dev))
            for c in cs:
                c.wait_recv()
            merged = [None, None]
            for axis, buf in ((0, xy), (1, xz)):
                part = axis ^ stage
                merged[part] = merge([buf[n, stage, q, 0:32, :] for q in range(4)])
                if extra is not None and part == 0:
                    more = total([buf[n, stage, q, 32:40, :] for q in range(4)])[0:1, 0:1]
            vals = merged
            extra = more if extra is not None else None
        return jnp.concatenate(vals, axis=0), extra

    turned = jnp.concatenate([wt_ref[...], jnp.ones((96, 128), jnp.float32)], axis=0).T
    wt = jnp.where(lane64 < 32, turned[0:64], pltpu.roll(turned[64:128], 32, 1))
    cap = cap_ref[...]
    wsum = jnp.sum(jnp.where(lane64 < 64, wt, 0.0), keepdims=True)
    csum = jnp.sum(cap, keepdims=True)
    logwt = jnp.log(wt)

    def col_first(f1, b, at, carry):
        f = column(f1, at)
        for k in range(KP):
            c = s_ref[b, :, ks(k)] + f
            m = jnp.max(c, axis=0, keepdims=True)
            tm_ref[rows_at(k, b), :] = m
            ts_ref[rows_at(k, b), :] = jnp.sum(jnp.exp(c - m), axis=0, keepdims=True)
        return carry

    f1 = rows_then_cols(0, score_block, csum, lse, lambda r: logwt - r, col_first)
    extra = slice(LANES // 2, LANES // 2 + 8)
    capacity = total([xrow[0, 0, q, extra, :] for q in range(8)])[0:1, 0:1]

    block = lax.broadcasted_iota(jnp.int32, (128, 128), 0)

    def spread_max(r, acc):
        for u in range(4):
            one = pl.ds(r * 4 + u, 1)
            acc = jnp.maximum(acc, jnp.where(block == tgt_ref[one, :], tm_ref[one, :], NEG))
        return acc

    peak = lax.fori_loop(0, 64, spread_max, jnp.full((128, 128), NEG, jnp.float32))
    peak = jnp.maximum(peak, pltpu.roll(peak, 64, 1))

    lanes = lax.broadcasted_iota(jnp.int32, (256, 128), 1)
    tgt = tgt_ref[...]
    hot = jnp.concatenate(
        [jnp.where(lanes == tgt[:, 0:1], 1.0, 0.0), jnp.where(lanes == tgt[:, 64:65], 1.0, 0.0)], axis=1
    )
    hot_t = jnp.concatenate(
        [hot[:, 0:128].T, hot[:, 128:256].T], axis=1
    ).astype(jnp.bfloat16)
    hot = hot.astype(jnp.bfloat16)

    def hot_dot(one, v):
        out = []
        for _ in range(3):
            h = v.astype(jnp.bfloat16).astype(jnp.float32)
            out.append(h)
            v = v - h
        w = jnp.concatenate(out, axis=1)
        side = (lax.broadcasted_iota(jnp.int32, (1, 384), 1) & 64) == 0
        w = jnp.concatenate([jnp.where(side, w, 0.0), jnp.where(side, 0.0, w)], axis=0)
        o = jnp.dot(one, w.astype(jnp.bfloat16), preferred_element_type=jnp.float32)
        return o[:, 0:128] + (o[:, 128:256] + o[:, 256:384])

    def spread_out(v):
        return hot_dot(hot, v)

    def collect(v):
        o = hot_dot(hot_t, v)
        return o + pltpu.roll(o, 64, 1)

    def compact(v):
        return jnp.where(left, v[0:64], v[64:128])

    def expand(c):
        r = pltpu.roll(c, 64, 1)
        return jnp.concatenate([jnp.where(left, c, r), jnp.where(left, r, c)], axis=0)

    tiles = ts_ref[...] * jnp.exp(tm_ref[...] - spread_out(peak))
    sums = collect(tiles)
    some = sums > 0.0
    col = jnp.where(some, peak + jnp.log(jnp.where(some, sums, 1.0)), NEG)
    col, weight = col_exchange(0, compact(col), wsum, lse)
    lw = jnp.log(weight)
    f1 = f1 - lw
    g1 = jnp.log(cap) - jnp.log(capacity) - (col - lw)
    amass = wt / weight
    bmass = cap / capacity

    tm_ref[...] = spread_out(expand(g1))

    def first_rows(b, at, acc):
        f = column(f1, at)
        t = None
        for k in range(KP):
            e = jnp.exp(s_ref[b, :, ks(k)] + f + tm_ref[rows_at(k, b), :])
            s_ref[b, :, ks(k)] = e
            t = e if t is None else t + e
        return jnp.where(lane64 == at, jnp.sum(t, axis=1, keepdims=True), acc)

    def cols(u, b, at, carry):
        c = column(u, at)
        for k in range(KP):
            ts_ref[rows_at(k, b), :] = jnp.sum(s_ref[b, :, ks(k)] * c, axis=0, keepdims=True)
        return carry

    u = rows_then_cols(1, first_rows, None, total, lambda r: amass / r, cols)
    v = bmass / col_exchange(1, compact(collect(ts_ref[...])), None, total)[0]

    tm_ref[...] = spread_out(expand(v))

    def rows(b, at, acc):
        t = functools.reduce(
            jnp.add, [s_ref[b, :, ks(k)] * tm_ref[rows_at(k, b), :] for k in range(KP)]
        )
        return jnp.where(lane64 == at, jnp.sum(t, axis=1, keepdims=True), acc)

    u = rows_then_cols(2, rows, None, total, lambda r: amass / r, cols)
    f = f1 + jnp.log(u)
    fout_ref[...] = jnp.concatenate([f, pltpu.roll(f, 96, 1)], axis=0).T[0:32]
    v = bmass / col_exchange(2, compact(collect(ts_ref[...])), None, total)[0]
    gout_ref[...] = g1 + jnp.log(v)

    for c in sends:
        c.wait_send()


def body(residuals, codebook, item_weight, code_capacity, pairs):
    items = residuals.shape[1]
    codes = codebook.shape[1]
    vm = pl.BlockSpec(memory_space=pltpu.VMEM)
    hbm = pl.BlockSpec(memory_space=pl.ANY)
    f32, bf16 = jnp.float32, jnp.bfloat16
    dma = pltpu.SemaphoreType.DMA
    f, g = pl.pallas_call(
        kernel,
        out_shape=[jax.ShapeDtypeStruct((32, 128), f32), jax.ShapeDtypeStruct((64, 128), f32)],
        in_specs=[hbm, hbm, vm, vm, hbm],
        out_specs=[vm, vm],
        scratch_shapes=[
            pltpu.VMEM((16, 2, 8, codes), f32),
            pltpu.VMEM((16, 16, items), f32),
            pltpu.VMEM((128, 16, 16, 128), bf16),
            pltpu.VMEM((128, 16, 16, 128), bf16),
            pltpu.VMEM((64, 128, 256), bf16),
            pltpu.VMEM((64, 64, 512), f32),
            pltpu.VMEM((16, 64), jnp.int32),
            pltpu.VMEM((128, 128), jnp.int32),
            pltpu.VMEM((256, 128), jnp.int32),
            pltpu.VMEM((64, 128), jnp.int32),
            pltpu.SMEM((64, 128), jnp.int32),
            pltpu.VMEM((256, 128), f32),
            pltpu.VMEM((256, 128), f32),
            pltpu.VMEM((3, PARTS, 8, LANES // 2 + 8, 128), f32),
            pltpu.VMEM((3, 2, 4, 40, 128), f32),
            pltpu.VMEM((3, 2, 4, 40, 128), f32),
            dma((64,)),
            dma((64,)),
            dma((8,)),
            dma((8,)),
            dma((4,)),
            dma((21 * PARTS,)),
            dma((21 * PARTS,)),
            dma((18,)),
            dma((18,)),
            dma((18,)),
            dma((18,)),
        ],
        compiler_params=pltpu.CompilerParams(
            collective_id=0, has_side_effects=True, vmem_limit_bytes=60 * 1024 * 1024
        ),
    )(
        codebook.reshape(2, 8, codes),
        residuals.reshape(2, 16, items),
        item_weight.reshape(32, 128),
        code_capacity.reshape(64, 128),
        pairs.T,
    )
    return f.reshape(items), g.reshape(codes)


def solution(mesh):
    placed = (P("code", "item"), P("item", "code"), P("item"), P("code"), P("item", "code"))
    return jax.shard_map(
        body, mesh=mesh, in_specs=placed, out_specs=(P("item"), P("code")), check_vma=False
    )
```
